256 devices in a mesh: seq: 32 (over z_hi, x, y), head: 8 (over z_lo, core).
Axes of the slice: x: 4, y: 4, z: 8 (z_hi: 2, z_lo: 4; z = z_hi * 4 + z_lo), core: 2. Of those that a mesh axis runs over, the one named last changes fastest.
Arguments:
- tokens: bfloat16 [32, 1024, 3072], P('seq', None, 'head'), may hold values from -6 to 6
- fast_state: float32 [32, 8, 192, 2304], P('seq', 'head'), may hold values from -6 to 6
- momentum: float32 [32, 8, 192, 2304], P('seq', 'head'), may hold values from -1.8 to 1.8
- init_fast: bfloat16 [8, 192, 2304], P('head'), may hold values from -6 to 6
- past_keys: bfloat16 [32, 2048, 1536], P('seq', None, 'head'), may hold values from -6 to 6
- past_values: bfloat16 [32, 2048, 1536], P('seq', None, 'head'), may hold values from -6 to 6
- qkv_weight: bfloat16 [3, 3072, 1536], P(None, 'seq', 'head'), may hold values from -0.109375 to 0.109375
- rate_weight: bfloat16 [3072, 8], P(None, 'head'), may hold values from -0.109375 to 0.109375
- out_weight: bfloat16 [1536, 3072], P('head'), may hold values from -0.15625 to 0.15625
- prompt_begins: int32 [2, 32], replicated, may hold values 0 or 1
Outputs:
- mixed: bfloat16 [32, 1024, 3072], P('seq', None, 'head')
- fast_out: float32 [32, 8, 192, 2304], P('seq', 'head')
- momentum_out: float32 [32, 8, 192, 2304], P('seq', 'head')
The draws below stay inside these ranges and needn't reach their ends.
All inputs are finite; a program needn't handle non-finite values.
Results may differ from the reference program's by a relative error of at most 0.015.
Values may be sent and summed in bfloat16 or wider, within the bound.
No kernel may reach another device: no remote copies, remote signals or barrier semaphores. Data moves between devices by JAX's collectives and lax.ppermute only.
A program may use at most 128 MiB of HBM per device.

```python
import math
import jax
import jax.numpy as jnp
from jax import lax

D = 3072
HEADS = 8
HD = 192
HID = 768
SPAN = 512
WINDOW = 2048
STEPS = 2
POSITIONS = 32
N_HEAD = 8


def plant(drawn, own_key, low, top_value):
    longest = drawn.shape.index(max(drawn.shape))
    spots = []
    for shift in (0, 1):
        where = [jax.random.randint(jax.random.fold_in(own_key, axis), (), 0, length) for axis, length in enumerate(drawn.shape)]
        where[longest] = (where[longest] + shift) % drawn.shape[longest]
        spots.append(tuple(where))
    return drawn.at[spots[0]].set(low).at[spots[1]].set(top_value)


def block_levels(own_key, extent, pieces, least, top_value):
    def one(position, shards_of):
        steps = jax.random.uniform(jax.random.fold_in(jax.random.fold_in(own_key, 6), position), (shards_of,), jnp.float32, least / len(pieces), top_value / len(pieces))
        return jnp.repeat(jnp.exp(steps), extent[position] // shards_of).reshape((-1,) + (1,) * (len(extent) - position - 1))

    loudness = one(*pieces[0])
    for cut in pieces[1:]:
        loudness = loudness * one(*cut)
    return loudness


def noise(stream_key, shape, width, reach, cuts=(), kind=jnp.bfloat16):
    values = jax.random.normal(stream_key, shape, jnp.float32) * width
    if len(cuts) > 0:
        values = block_levels(stream_key, shape, cuts, -0.22, 0.18) * values
    return jnp.clip(values, min=-reach, max=reach).astype(kind)


def setup_inputs(seed: int = 0) -> dict:
    arg_keys = jax.random.split(jax.random.key(seed), 11)
    tokens = noise(arg_keys[0], (POSITIONS, STEPS * SPAN, D), 1.0, 6.0, ((0, 32), (2, 8)))
    fast_state = noise(arg_keys[1], (POSITIONS, HEADS, HD, 3 * HID), 1.0, 6.0, ((0, 32), (1, 8)), jnp.float32)
    momentum = noise(arg_keys[2], (POSITIONS, HEADS, HD, 3 * HID), 0.3, 1.8, ((0, 32), (1, 8)), jnp.float32)
    init_fast = noise(arg_keys[3], (HEADS, HD, 3 * HID), 1.0, 6.0, ((0, 8),))
    past_keys = noise(arg_keys[4], (POSITIONS, WINDOW, HEADS * HD), 1.0, 6.0, ((0, 32), (2, 8)))
    past_values = noise(arg_keys[5], (POSITIONS, WINDOW, HEADS * HD), 1.0, 6.0, ((0, 32), (2, 8)))
    qkv_weight = noise(arg_keys[6], (3, D, HEADS * HD), D ** -0.5, 0.109375, ((1, 32), (2, 8)))
    rate_weight = noise(arg_keys[7], (D, HEADS), D ** -0.5, 0.109375, ((1, 8),))
    out_weight = noise(arg_keys[8], (HEADS * HD, D), (HEADS * HD) ** -0.5, 0.15625, ((0, 8),))
    prompt_begins = plant((jax.random.randint(arg_keys[9], (STEPS, POSITIONS), 0, 4) < 1).astype(jnp.int32), jax.random.fold_in(arg_keys[9], 1), 0, 1)
    return dict(tokens=tokens, fast_state=fast_state, momentum=momentum, init_fast=init_fast, past_keys=past_keys, past_values=past_values, qkv_weight=qkv_weight, rate_weight=rate_weight, out_weight=out_weight, prompt_begins=prompt_begins)


momentum_decay = 0.9
rate_scale = 0.3
epsilon = 1e-06
highest = lax.Precision.HIGHEST

def unit_rows(matrix):
    return matrix * lax.rsqrt(lax.optimization_barrier(jnp.mean(matrix * matrix, axis=-1, keepdims=True)) + epsilon)

def head_span(queries, keys_span, values_span, step_size, window_keys, window_values, visible_prev, restart, weights_now, momentum_now, initial):
    span_len = queries.shape[0]
    window_len = window_keys.shape[0]
    head_dim = queries.shape[1]
    hidden = weights_now.shape[1] // 3
    score_bound = math.sqrt(head_dim)
    query_unit = unit_rows(queries.astype(jnp.float32))
    key_unit = unit_rows(keys_span.astype(jnp.float32))
    context_keys = jnp.concatenate([unit_rows(window_keys.astype(jnp.float32)), key_unit], axis=0).astype(jnp.bfloat16)
    context_values = jnp.concatenate([window_values, values_span], axis=0)
    scores = lax.dot_general(query_unit.astype(jnp.bfloat16), context_keys, (((1,), (1,)), ((), ())), preferred_element_type=jnp.float32) / score_bound
    query_pos = lax.broadcasted_iota(jnp.int32, scores.shape, 0)
    key_pos = lax.broadcasted_iota(jnp.int32, scores.shape, 1)
    restart_flag = restart.astype(jnp.float32)
    keep_prev = jnp.concatenate([visible_prev * (1.0 - restart_flag), jnp.ones((span_len,), jnp.float32)])
    inside = (key_pos > query_pos) & (key_pos <= query_pos + window_len)
    soft_weights = jnp.where(inside, jnp.exp(scores - score_bound), 0.0) * keep_prev[None, :]
    denominator = lax.optimization_barrier(jnp.sum(soft_weights, axis=1, keepdims=True))
    attended = jnp.dot(soft_weights.astype(jnp.bfloat16), context_values, preferred_element_type=jnp.float32) / denominator
    weights_now = jnp.where(restart > 0, initial.astype(jnp.float32), weights_now)
    momentum_now = jnp.where(restart > 0, jnp.zeros_like(momentum_now), momentum_now)
    up_proj = weights_now[:, :2 * hidden]
    down_proj = weights_now[:, 2 * hidden:]
    hidden_scale = math.sqrt(hidden)
    query_in = query_unit / score_bound
    key_in = key_unit / score_bound
    both_in = jnp.dot(query_in, up_proj, precision=highest, preferred_element_type=jnp.float32)
    mixed_hidden = jax.nn.silu(both_in[:, :hidden]) * both_in[:, hidden:]
    applied = lax.dot_general(mixed_hidden, down_proj, (((1,), (1,)), ((), ())), precision=highest, preferred_element_type=jnp.float32) / hidden_scale
    both_key = jnp.dot(key_in, up_proj, precision=highest, preferred_element_type=jnp.float32)
    gate_key = both_key[:, :hidden]
    lift_key = both_key[:, hidden:]
    gate_sigmoid = jax.nn.sigmoid(gate_key)
    gate_silu = gate_key * gate_sigmoid
    hidden_key = gate_silu * lift_key
    out_grad = -step_size.astype(jnp.float32)[:, None] * values_span.astype(jnp.float32)
    down_grad = lax.dot_general(out_grad, hidden_key, (((0,), (0,)), ((), ())), precision=highest, preferred_element_type=jnp.float32) / hidden_scale
    hidden_grad = jnp.dot(out_grad, down_proj, precision=highest, preferred_element_type=jnp.float32) / hidden_scale
    gate_grad = hidden_grad * lift_key * gate_sigmoid * (1.0 + gate_key * (1.0 - gate_sigmoid))
    lift_grad = hidden_grad * gate_silu
    up_grad = lax.dot_general(key_in, jnp.concatenate([gate_grad, lift_grad], axis=1), (((0,), (0,)), ((), ())), precision=highest, preferred_element_type=jnp.float32)
    gradient = jnp.concatenate([up_grad, down_grad], axis=1)
    momentum_new = momentum_decay * momentum_now + gradient
    stepped = weights_now - momentum_new
    weights_new = stepped * lax.rsqrt(lax.optimization_barrier(jnp.mean(stepped * stepped, axis=0, keepdims=True)) + epsilon)
    head_mix = (attended + applied).astype(jnp.bfloat16)
    return (head_mix, weights_new, momentum_new)

def position_span(queries, keys_span, values_span, step_size, window_keys, window_values, visible_prev, restart, weights_now, momentum_now, initial):
    heads_here = weights_now.shape[0]

    def split_heads(matrix):
        return matrix.reshape(matrix.shape[0], heads_here, matrix.shape[1] // heads_here)
    mapped = jax.vmap(head_span, in_axes=(1, 1, 1, 1, 1, 1, None, None, 0, 0, 0), out_axes=(1, 0, 0))
    head_mix, weights_new, momentum_new = mapped(split_heads(queries), split_heads(keys_span), split_heads(values_span), step_size, split_heads(window_keys), split_heads(window_values), visible_prev, restart, weights_now, momentum_now, initial)
    return (head_mix.reshape(head_mix.shape[0], -1), weights_new, momentum_new)

def next_window(window_keys, window_values, visible_prev, restart, keys_span, values_span):
    window_len = window_keys.shape[0]
    kept_rows = visible_prev * (1.0 - restart.astype(visible_prev.dtype))
    fresh_rows = jnp.ones((keys_span.shape[0],), visible_prev.dtype)
    new_keys = jnp.concatenate([window_keys, keys_span], axis=0)[-window_len:]
    new_values = jnp.concatenate([window_values, values_span], axis=0)[-window_len:]
    new_visible = jnp.concatenate([kept_rows, fresh_rows])[-window_len:]
    return (new_keys, new_values, new_visible)

def reference(tokens, fast_state, momentum, init_fast, past_keys, past_values, qkv_weight, rate_weight, out_weight, prompt_begins):
    positions = tokens.shape[0]

    def project(token_rows):
        query_all = jnp.dot(token_rows, qkv_weight[0], preferred_element_type=jnp.float32).astype(jnp.bfloat16)
        key_all = jnp.dot(token_rows, qkv_weight[1], preferred_element_type=jnp.float32).astype(jnp.bfloat16)
        value_all = jnp.dot(token_rows, qkv_weight[2], preferred_element_type=jnp.float32).astype(jnp.bfloat16)
        rates = (rate_scale * jax.nn.softplus(jnp.dot(token_rows, rate_weight, preferred_element_type=jnp.float32))).astype(jnp.bfloat16)
        return (query_all, key_all, value_all, rates)
    queries, keys_all, values_all, step_sizes = lax.map(project, tokens)
    weights_now = fast_state
    momentum_now = momentum
    window_keys = past_keys
    window_values = past_values
    visible = jnp.ones((positions, WINDOW), jnp.float32)
    mix_blocks = []

    def one_position(packed):
        return position_span(*packed, init_fast)
    for section_index in range(STEPS):
        first_row = section_index * SPAN
        last_row = first_row + SPAN
        restart = prompt_begins[section_index]
        span_keys = keys_all[:, first_row:last_row]
        span_values = values_all[:, first_row:last_row]
        head_mix, weights_new, momentum_new = lax.map(one_position, (queries[:, first_row:last_row], span_keys, span_values, step_sizes[:, first_row:last_row], window_keys, window_values, visible, restart, weights_now, momentum_now))
        window_keys, window_values, visible = jax.vmap(next_window)(window_keys, window_values, visible, restart, span_keys, span_values)
        mix_blocks.append(head_mix)
        if section_index + 1 < STEPS:
            weights_now = jnp.roll(weights_new, 1, axis=0)
            momentum_now = jnp.roll(momentum_new, 1, axis=0)
            window_keys = jnp.roll(window_keys, 1, axis=0)
            window_values = jnp.roll(window_values, 1, axis=0)
            visible = jnp.roll(visible, 1, axis=0)
        else:
            weights_now = weights_new
            momentum_now = momentum_new
    head_rows_all = jnp.concatenate(mix_blocks, axis=1)
    group_width = HEADS // N_HEAD * HD

    def project_out(head_rows):
        running = jnp.zeros((head_rows.shape[0], out_weight.shape[1]), jnp.float32)
        for group_index in range(N_HEAD):
            lower = group_index * group_width
            partial_value = jnp.dot(head_rows[:, lower:lower + group_width], out_weight[lower:lower + group_width], preferred_element_type=jnp.float32).astype(jnp.bfloat16)
            partial_value = lax.optimization_barrier(partial_value)
            running = running + partial_value.astype(jnp.float32)
        return running.astype(jnp.bfloat16)
    mixed = lax.map(project_out, head_rows_all)
    return (mixed, weights_now, momentum_now)
```

```python
import math

import jax
import jax.numpy as jnp
from jax import lax
from jax.experimental import pallas as pl
from jax.experimental.pallas import tpu as pltpu
from jax.sharding import PartitionSpec as P

SPAN = 512
WINDOW = 2048
HD = 192
HID = 768
SHARD = 96
WIDE = 640
BLOCK = 384
AXES = ("seq", "head")
EPS = 1e-06
LOG2E = 1.4426950408889634
SCORE = math.sqrt(HD)
ROOT_HID = math.sqrt(HID)
BF = jnp.bfloat16
F32 = jnp.float32
VMEM = pl.BlockSpec(memory_space=pltpu.VMEM)
SMEM = pl.BlockSpec(memory_space=pltpu.SMEM)


def pairs(target):
    out = []
    for i in range(256):
        s, h = i // 8, i % 8
        goal = target(s // 16, (s // 4) % 4, s % 4, h // 2, h % 2)
        if goal is not None:
            zh, x, y, zl, c = goal
            out.append((i, ((zh * 4 + x) * 4 + y) * 8 + zl * 2 + c))
    return out


def step_pairs(distance):
    return [(i, ((i // 8 + distance) % 32) * 8 + i % 8) for i in range(256)]


CORE = pairs(lambda zh, x, y, zl, c: (zh, x, y, zl, 1 - c))
ZL1 = pairs(lambda zh, x, y, zl, c: (zh, x, y, zl ^ 1, c))
ZL2 = pairs(lambda zh, x, y, zl, c: (zh, x, y, zl ^ 2, c))
ZL3 = pairs(lambda zh, x, y, zl, c: (zh, x, y, zl ^ 3, c))
ZH = pairs(lambda zh, x, y, zl, c: (1 - zh, x, y, zl, c))
XS = [pairs(lambda zh, x, y, zl, c, k=k: (zh, (x + k) % 4, y, zl, c)) for k in range(4)]
YS = [pairs(lambda zh, x, y, zl, c, k=k: (zh, x, (y + k) % 4, zl, c)) for k in range(4)]
FORWARD = step_pairs(1)
BACK = step_pairs(-1)


def move(array, route):
    return lax.ppermute(array, AXES, route)


def gather_heads(block):
    one = move(block, ZL1)
    two = move(block, ZL2)
    near = move(block, CORE)
    three = move(two, ZL1)
    return [
        block,
        near,
        one,
        move(one, CORE),
        two,
        move(two, CORE),
        three,
        move(three, CORE),
    ]


def matmul(a, b):
    return jnp.dot(a, b, preferred_element_type=F32)


def matmul_nt(a, b):
    return lax.dot_general(a, b, (((1,), (1,)), ((), ())), preferred_element_type=F32)


def unit(rows):
    return rows * lax.rsqrt(jnp.mean(rows * rows, axis=-1, keepdims=True) + EPS)


def sigmoid(a):
    return 1.0 / (1.0 + jnp.exp(-a))


def with_ones(values):
    rows = values.shape[0]
    lane = lax.broadcasted_iota(jnp.int32, (rows, 64), 1)
    return jnp.concatenate([values.astype(F32), jnp.where(lane == 0, 1.0, 0.0)], axis=1).astype(BF)


def call(kernel, outs, *args, flops=0, moved=0, scratch=(), limit=40):
    return pl.pallas_call(
        kernel,
        out_shape=outs,
        in_specs=[SMEM] + [VMEM] * (len(args) - 1),
        out_specs=jax.tree.map(lambda _: VMEM, outs),
        scratch_shapes=list(scratch),
        compiler_params=pltpu.CompilerParams(vmem_limit_bytes=limit * 1024 * 1024),
        cost_estimate=pl.CostEstimate(flops=flops, bytes_accessed=moved, transcendentals=0),
    )(*args)


def shape(*dims, dtype=BF):
    return jax.ShapeDtypeStruct(dims, dtype)


def prepare_window(scalars, keys, values, unit_keys, wide_values):
    for at in range(0, WINDOW, 512):
        rows = slice(at, at + 512)
        unit_keys[rows, :] = unit(keys[rows, :].astype(F32)).astype(BF)
        wide_values[rows, :] = with_ones(values[rows, :])


def finish_projection(product, queries, keys_grads, values_wide):
    q = product[:, :HD].astype(BF).astype(F32)
    k = product[:, HD : 2 * HD].astype(BF).astype(F32)
    v = product[:, 2 * HD : 3 * HD].astype(BF)
    rate = product[:, 3 * HD : 3 * HD + 1]
    soft = jnp.maximum(rate, 0.0) + jnp.log(1.0 + jnp.exp(-jnp.abs(rate)))
    step = (0.3 * soft).astype(BF).astype(F32)
    grad = -step * v.astype(F32)
    queries[...] = unit(q).astype(BF)
    keys_grads[...] = jnp.concatenate([unit(k), grad], axis=1).astype(BF)
    values_wide[...] = with_ones(v)


def load_tokens(blocks, tokens):
    for b in range(8):
        tokens[:, b * BLOCK : (b + 1) * BLOCK] = blocks[b][...]


def project_first(scalars, *refs):
    blocks = refs[:8]
    pieces = refs[8:16]
    weights, queries, keys_grads, values_wide, tokens = refs[16:]
    seq = scalars[0]
    head = scalars[1]
    zh, x, y = seq // 16, (seq // 4) % 4, seq % 4
    for side in range(2):
        for outer in range(4):
            piece = pieces[side * 4 + outer]
            for inner in range(4):
                dx, dy = (outer, inner) if side == 0 else (inner, outer)
                from_x, from_y = (x + 4 - dx) % 4, (y + 4 - dy) % 4
                from_zh = zh if side == 0 else 1 - zh
                slot = (from_zh * 4 + from_x) ^ head
                row = pl.multiple_of((slot * 4 + from_y) * SHARD, SHARD)
                weights[pl.ds(row, SHARD), :] = piece[inner * SHARD : (inner + 1) * SHARD, :]
    load_tokens(blocks, tokens)
    product = matmul(tokens[...], weights[...])
    finish_projection(product, queries, keys_grads, values_wide)


def project_second(scalars, *refs):
    blocks = refs[:8]
    weights, queries, keys_grads, values_wide, tokens = refs[8:]
    load_tokens(blocks, tokens)
    product = matmul(tokens[...], weights[...])
    finish_projection(product, queries, keys_grads, values_wide)


def soft_weights(q, k, keep=None):
    scores = matmul_nt(q, k)
    soft = jnp.exp2(scores * (LOG2E / SCORE) - SCORE * LOG2E)
    if keep is not None:
        soft = jnp.where(keep, soft, 0.0)
    return soft.astype(BF)


def corner(row0, rows, cols, own):
    a = lax.broadcasted_iota(jnp.int32, (rows, cols), 0) + row0
    j = lax.broadcasted_iota(jnp.int32, (rows, cols), 1)
    return j <= a if own else j > a


def attend(q, row0, chunks):
    total = None
    for k, v, mask in chunks:
        keep = None if mask is None else corner(row0, q.shape[0], k.shape[0], mask == "own")
        part = matmul(soft_weights(q, k, keep), v)
        total = part if total is None else total + part
    return total


def fast_read(q, weights):
    total = None
    for at in range(0, HID, 256):
        gate = matmul(q, weights(at)) * (1.0 / SCORE)
        lift = matmul(q, weights(HID + at)) * (1.0 / SCORE)
        hidden = (gate * sigmoid(gate) * lift).astype(BF)
        part = matmul_nt(hidden, weights(2 * HID + at))
        total = part if total is None else total + part
    return total * (1.0 / ROOT_HID)


def fast_write(keys_grads, weights, momentum, weights_out, momentum_out):
    y = keys_grads[:, :HD]
    g = keys_grads[:, HD:]
    y_turned = y.astype(F32).T.astype(BF)
    g_turned = g.astype(F32).T.astype(BF)
    for at in range(0, HID, 256):
        spots = (at, HID + at, 2 * HID + at)
        now = [weights(spot) for spot in spots]
        u1, u3, p = (w.astype(BF) for w in now)
        gate = matmul(y, u1) * (1.0 / SCORE)
        lift = matmul(y, u3) * (1.0 / SCORE)
        err = matmul(g, p) * (1.0 / ROOT_HID)
        sg = sigmoid(gate)
        silu = gate * sg
        gate_grad = (err * lift * sg * (1.0 + gate * (1.0 - sg))).astype(BF)
        lift_grad = (err * silu).astype(BF)
        hidden = (silu * lift).astype(BF)
        grads = (
            matmul(y_turned, gate_grad) * (1.0 / SCORE),
            matmul(y_turned, lift_grad) * (1.0 / SCORE),
            matmul(g_turned, hidden) * (1.0 / ROOT_HID),
        )
        for spot, w, grad in zip(spots, now, grads):
            m = 0.9 * momentum(spot) + grad
            stepped = w - m
            scale = lax.rsqrt(jnp.mean(stepped * stepped, axis=0, keepdims=True) + EPS)
            weights_out(spot, stepped * scale)
            momentum_out(spot, m)


def first_mix(scalars, queries, keys_grads, values, past_keys, past_values, fast, initial, mix):
    fresh = scalars[2] > 0
    seen = jnp.where(fresh, 0.0, 1.0)
    for row in range(0, SPAN, 256):
        q = queries[row : row + 256, :]
        past = attend(
            q,
            row,
            [
                (
                    past_keys[at : at + 512, :],
                    past_values[at : at + 512, :],
                    "past" if at == 0 else None,
                )
                for at in range(0, WINDOW, 512)
            ],
        )
        own = attend(q, row, [(keys_grads[:, :HD], values[...], "own")])
        total = past * seen + own
        attended = total[:, :HD] / total[:, HD : HD + 1]
        applied = fast_read(
            q,
            lambda at: jnp.where(
                fresh, initial[:, at : at + 256].astype(F32), fast[:, at : at + 256]
            ).astype(BF),
        )
        mix[row : row + 256, :] = (attended + applied).astype(BF)


def lend_window(scalars, queries, past_keys, past_values, keys_grads, values, part):
    old = jnp.where(scalars[2] > 0, 0.0, 1.0)
    seen = jnp.where(scalars[5] > 0, 0.0, 1.0)
    for row in range(0, SPAN, 256):
        q = queries[row : row + 256, :]
        past = attend(
            q,
            row,
            [
                (
                    past_keys[at : at + 512, :],
                    past_values[at : at + 512, :],
                    "past" if at == 512 else None,
                )
                for at in range(512, WINDOW, 512)
            ],
        )
        new = attend(q, row, [(keys_grads[:, :HD], values[...], None)])
        total = (past * old + new) * seen
        weight = total[:, HD : HD + 1]
        high = weight.astype(BF).astype(F32)
        lane = lax.broadcasted_iota(jnp.int32, (256, 64), 1)
        tail = jnp.where(lane == 0, high, jnp.where(lane == 1, weight - high, 0.0))
        part[row : row + 256, :] = jnp.concatenate([total[:, :HD], tail], axis=1).astype(BF)


def arrive_state(scalars, keys_grads, fast, momentum, initial, fast_out, momentum_out):
    fresh_before = scalars[4] > 0
    fresh = scalars[3] > 0

    def weights(at):
        return jnp.where(
            fresh_before,
            initial[:, at : at + 256].astype(F32),
            fast[:, at : at + 256].astype(F32),
        )

    def moment(at):
        return jnp.where(fresh_before, 0.0, momentum[:, at : at + 256].astype(F32))

    def keep_weights(at, value):
        fast_out[:, at : at + 256] = jnp.where(
            fresh, initial[:, at : at + 256].astype(F32), value
        )

    def keep_moment(at, value):
        momentum_out[:, at : at + 256] = jnp.where(fresh, 0.0, value)

    fast_write(keys_grads, weights, moment, keep_weights, keep_moment)


def second_mix(scalars, queries, keys_grads, values, fast, part, mix):
    for row in range(0, SPAN, 256):
        rows = slice(row, row + 256)
        q = queries[rows, :]
        total = attend(q, row, [(keys_grads[:, :HD], values[...], "own")])
        lent = part[rows, :].astype(F32)
        weight = total[:, HD : HD + 1] + lent[:, HD : HD + 1] + lent[:, HD + 1 : HD + 2]
        attended = (total[:, :HD] + lent[:, :HD]) / weight
        applied = fast_read(q, lambda at: fast[:, at : at + 256].astype(BF))
        mix[rows, :] = (attended + applied).astype(BF)


def last_state(scalars, keys_grads, fast, momentum, fast_out, momentum_out):
    def keep_weights(at, value):
        fast_out[:, at : at + 256] = value

    def keep_moment(at, value):
        momentum_out[:, at : at + 256] = value

    fast_write(
        keys_grads,
        lambda at: fast[:, at : at + 256],
        lambda at: momentum[:, at : at + 256],
        keep_weights,
        keep_moment,
    )


def project_out(scalars, *refs):
    blocks = refs[:8]
    mine, other, out = refs[8:]
    total = None
    for b in range(8):
        weights = (mine if b % 2 == 0 else other)[b // 2]
        part = matmul(blocks[b][...], weights)
        total = part if total is None else total + part
    out[...] = total.astype(BF)


def body(
    tokens,
    fast_state,
    momentum,
    init_fast,
    past_keys,
    past_values,
    qkv_weight,
    rate_weight,
    out_weight,
    prompt_begins,
):
    seq = lax.axis_index("seq")
    head = lax.axis_index("head")
    zl, core = head // 2, head % 2
    scalars = jnp.stack(
        [
            seq,
            head,
            prompt_begins[0, seq],
            prompt_begins[1, seq],
            prompt_begins[0, (seq + 31) % 32],
            prompt_begins[1, (seq + 1) % 32],
        ]
    ).astype(jnp.int32)

    shard = jnp.concatenate(
        [
            qkv_weight[0],
            qkv_weight[1],
            qkv_weight[2],
            lax.dynamic_slice(rate_weight, (seq * SHARD, 0), (SHARD, 1)),
            jnp.zeros((SHARD, WIDE - 3 * HD - 1), BF),
        ],
        axis=1,
    )
    across = move(shard, ZH)
    first_tokens = gather_heads(tokens[0, :SPAN])
    rows_y = jnp.concatenate([shard] + [move(shard, YS[k]) for k in (1, 2, 3)], axis=0)
    rows_x = jnp.concatenate([across] + [move(across, XS[k]) for k in (1, 2, 3)], axis=0)
    pieces = [rows_y] + [move(rows_y, XS[k]) for k in (1, 2, 3)]
    pieces += [rows_x] + [move(rows_x, YS[k]) for k in (1, 2, 3)]

    fast_sent = move(fast_state[0, 0].astype(BF), FORWARD)
    momentum_sent = move(momentum[0, 0].astype(BF), FORWARD)
    second_tokens = gather_heads(tokens[0, SPAN:])

    out_parts = [lax.dynamic_slice(out_weight, (0, zl * 768), (HD, 768))]
    for k, route in ((1, ZL1), (2, ZL2), (3, ZL3)):
        out_parts.append(
            move(lax.dynamic_slice(out_weight, (0, (zl ^ k) * 768), (HD, 768)), route)
        )
    out_parts = jnp.stack(out_parts)
    out_mine = lax.dynamic_slice(out_parts, (0, 0, core * BLOCK), (4, HD, BLOCK))
    out_other = move(
        lax.dynamic_slice(out_parts, (0, 0, (1 - core) * BLOCK), (4, HD, BLOCK)), CORE
    )

    unit_keys, wide_values = call(
        prepare_window,
        (shape(WINDOW, HD), shape(WINDOW, 256)),
        scalars,
        past_keys[0],
        past_values[0],
        moved=4 << 20,
    )
    span_outs = (shape(SPAN, HD), shape(SPAN, 2 * HD), shape(SPAN, 256))
    token_room = [pltpu.VMEM((SPAN, 8 * BLOCK), BF)]
    weights, q0, kg0, v0 = call(
        project_first,
        (shape(8 * BLOCK, WIDE),) + span_outs,
        scalars,
        *first_tokens,
        *pieces,
        flops=2 * SPAN * 3072 * WIDE,
        moved=12 << 20,
        scratch=token_room,
    )
    kg_before = move(kg0, FORWARD)
    mix0 = call(
        first_mix,
        shape(SPAN, HD),
        scalars,
        q0,
        kg0,
        v0,
        unit_keys,
        wide_values,
        fast_state[0, 0],
        init_fast[0],
        flops=4 << 30,
        moved=6 << 20,
    )
    mix0_all = gather_heads(mix0)
    q1, kg1, v1 = call(
        project_second,
        span_outs,
        scalars,
        *second_tokens,
        weights,
        flops=2 * SPAN * 3072 * WIDE,
        moved=8 << 20,
        scratch=token_room,
    )
    q_next = move(q1, BACK)
    part = call(
        lend_window,
        shape(SPAN, 256),
        scalars,
        q_next,
        unit_keys,
        wide_values,
        kg0,
        v0,
        flops=3 << 30,
        moved=3 << 20,
    )
    part_before = move(part, FORWARD)
    state = shape(HD, 3 * HID, dtype=F32)
    fast1, momentum1 = call(
        arrive_state,
        (state, state),
        scalars,
        kg_before,
        fast_sent,
        momentum_sent,
        init_fast[0],
        flops=3 << 30,
        moved=6 << 20,
    )
    mix1 = call(
        second_mix,
        shape(SPAN, HD),
        scalars,
        q1,
        kg1,
        v1,
        fast1,
        part_before,
        flops=2 << 30,
        moved=3 << 20,
    )
    mix1_all = gather_heads(mix1)
    fast2, momentum2 = call(
        last_state,
        (state, state),
        scalars,
        kg1,
        fast1,
        momentum1,
        flops=3 << 30,
        moved=8 << 20,
    )
    outs = [
        call(
            project_out,
            shape(SPAN, BLOCK),
            scalars,
            *blocks,
            out_mine,
            out_other,
            flops=2 * SPAN * 1536 * BLOCK,
            moved=4 << 20,
        )
        for blocks in (mix0_all, mix1_all)
    ]
    mixed = jnp.concatenate(outs, axis=0)
    return mixed[None], fast2[None, None], momentum2[None, None]


def solution(mesh):
    in_specs = (
        P("seq", None, "head"),
        P("seq", "head", None, None),
        P("seq", "head", None, None),
        P("head", None, None),
        P("seq", None, "head"),
        P("seq", None, "head"),
        P(None, "seq", "head"),
        P(None, "head"),
        P("head", None),
        P(),
    )
    out_specs = (P("seq", None, "head"), P("seq", "head", None, None), P("seq", "head", None, None))
    return jax.shard_map(body, mesh=mesh, in_specs=in_specs, out_specs=out_specs, check_vma=False)
```

```python
import math

import jax
import jax.numpy as jnp
from jax import lax
from jax.experimental import pallas as pl
from jax.experimental.pallas import tpu as pltpu
from jax.sharding import Mesh, PartitionSpec as P

SPAN = 512
WINDOW = 2048
HD = 192
HID = 768
SHARD = 96
WIDE = 640
BLOCK = 384
SEQ = ("zh", "xy")
AXES = ("zh", "xy", "head")
EPS = 1e-06
LOG2E = 1.4426950408889634
SCORE = math.sqrt(HD)
ROOT_HID = math.sqrt(HID)
BF = jnp.bfloat16
F32 = jnp.float32
VMEM = pl.BlockSpec(memory_space=pltpu.VMEM)
SMEM = pl.BlockSpec(memory_space=pltpu.SMEM)
ANY = pl.BlockSpec(memory_space=pl.ANY)


def pairs(target):
    out = []
    for i in range(256):
        s, h = i // 8, i % 8
        goal = target(s // 16, (s // 4) % 4, s % 4, h // 2, h % 2)
        if goal is not None:
            zh, x, y, zl, c = goal
            out.append((i, ((zh * 4 + x) * 4 + y) * 8 + zl * 2 + c))
    return out


def step_pairs(distance):
    return [(i, ((i // 8 + distance) % 32) * 8 + i % 8) for i in range(256)]


CORE = pairs(lambda zh, x, y, zl, c: (zh, x, y, zl, 1 - c))
ZL1 = pairs(lambda zh, x, y, zl, c: (zh, x, y, zl ^ 1, c))
ZL2 = pairs(lambda zh, x, y, zl, c: (zh, x, y, zl ^ 2, c))
ZL3 = pairs(lambda zh, x, y, zl, c: (zh, x, y, zl ^ 3, c))
ZH = pairs(lambda zh, x, y, zl, c: (1 - zh, x, y, zl, c))
XS = [pairs(lambda zh, x, y, zl, c, k=k: (zh, (x + k) % 4, y, zl, c)) for k in range(4)]
YS = [pairs(lambda zh, x, y, zl, c, k=k: (zh, x, (y + k) % 4, zl, c)) for k in range(4)]
FORWARD = step_pairs(1)
BACK = step_pairs(-1)


def move(array, route):
    return lax.ppermute(array, AXES, route)


def gather_tokens(block):
    near = move(block, CORE)
    one = move(block, ZL1)
    two = move(block, ZL2)
    three = move(two, ZL1)
    return [block, near, one, move(one, CORE), two, move(two, CORE), three, move(three, CORE)]


def matmul(a, b):
    return jnp.dot(a, b, preferred_element_type=F32)


def matmul_nt(a, b):
    return lax.dot_general(a, b, (((1,), (1,)), ((), ())), preferred_element_type=F32)


def unit(rows):
    return rows * lax.rsqrt(jnp.mean(rows * rows, axis=-1, keepdims=True) + EPS)


def sigmoid(a):
    return 1.0 / (1.0 + jnp.exp(-a))


def with_ones(values):
    rows = values.shape[0]
    lane = lax.broadcasted_iota(jnp.int32, (rows, 64), 1)
    return jnp.concatenate([values.astype(F32), jnp.where(lane == 0, 1.0, 0.0)], axis=1).astype(BF)


def call(kernel, outs, *args, flops=0, moved=0, scratch=(), limit=40, after=0, place=VMEM):
    return pl.pallas_call(
        kernel,
        out_shape=outs,
        in_specs=[SMEM] + [VMEM] * (len(args) - 1 - after) + [ANY] * after,
        out_specs=jax.tree.map(lambda _: place, outs),
        scratch_shapes=list(scratch),
        compiler_params=pltpu.CompilerParams(vmem_limit_bytes=limit * 1024 * 1024),
        cost_estimate=pl.CostEstimate(flops=flops, bytes_accessed=moved, transcendentals=0),
    )(*args)


def shape(*dims, dtype=BF):
    return jax.ShapeDtypeStruct(dims, dtype)


def prepare_window(begins, keys, values, unit_keys, wide_values):
    k = keys[...].astype(F32)
    unit_keys[...] = (k * lax.rsqrt(jnp.mean(k * k, axis=0, keepdims=True) + EPS)).astype(BF)
    wide_values[:HD, :] = values[...]
    row = lax.broadcasted_iota(jnp.int32, (64, WINDOW), 0)
    wide_values[HD:, :] = jnp.where(row == 0, 1.0, 0.0).astype(BF)


def build_shard(begins, weight, out):
    for c in range(3):
        out[:, c * HD : (c + 1) * HD] = weight[c]
    out[:, 3 * HD :] = jnp.zeros((SHARD, WIDE - 3 * HD), BF)


def join(begins, *refs):
    out = refs[-1]
    rows = refs[0].shape[0]
    for b, ref in enumerate(refs[:-1]):
        out[b * rows : (b + 1) * rows, :] = ref[...]


def copy_rows(begins, rows, done, out):
    out[...] = rows[...]


def pack_state(begins, fast, momentum, out):
    for b in range(8):
        out[b] = fast[24 * b : 24 * (b + 1), :].astype(BF)
        out[8 + b] = momentum[24 * b : 24 * (b + 1), :].astype(BF)


def turn(begins, shares, other, done, done_too, out):
    out[0] = other[...]
    for b in range(15):
        out[b + 1] = shares[b]


def split_out(begins, weight, *refs):
    outs = refs[3:]
    zl = lax.axis_index("head") // 2
    for k in range(4):
        at = pl.multiple_of((zl ^ k) * 2 * BLOCK, 2 * BLOCK)
        outs[k][...] = weight[:, pl.ds(at, 2 * BLOCK)]


def sort_out(begins, *refs):
    mine, theirs = refs[5:]
    core = lax.axis_index("head") % 2
    for k in range(4):
        rows = slice(k * HD, (k + 1) * HD)
        for out, side in ((mine, core), (theirs, 1 - core)):
            out[rows, :] = refs[k][:, pl.ds(pl.multiple_of(side * BLOCK, BLOCK), BLOCK)]


def collect(begins, one, two, three, done, out):
    out[0] = one[...]
    out[1] = two[...]
    out[2] = three[...]


def finish_projection(tokens, weights, rates, queries, keys_grads, values_wide):
    product = matmul(tokens, weights)
    rate = matmul_nt(tokens, rates)[:, :1]
    q = product[:, :HD].astype(BF).astype(F32)
    k = product[:, HD : 2 * HD].astype(BF).astype(F32)
    v = product[:, 2 * HD : 3 * HD].astype(BF)
    soft = jnp.maximum(rate, 0.0) + jnp.log(1.0 + jnp.exp(-jnp.abs(rate)))
    step = (0.3 * soft).astype(BF).astype(F32)
    grad = -step * v.astype(F32)
    queries[...] = unit(q).astype(BF)
    keys_grads[...] = jnp.concatenate([unit(k), grad], axis=1).astype(BF)
    values_wide[...] = with_ones(v)


def load_tokens(blocks, first, tokens):
    for b, block in enumerate(blocks):
        tokens[:, b * BLOCK : (b + 1) * BLOCK] = block[first : first + SPAN, :]


def project_first(begins, rate, *refs):
    blocks = refs[:8]
    pieces = refs[8:13]
    weights, rates, queries, keys_grads, values_wide, tokens = refs[13:]
    seq, head = lax.axis_index(SEQ), lax.axis_index("head")
    zh, x, y = seq // 16, (seq // 4) % 4, seq % 4
    for dx, piece, base in zip((0, 1, 3, 2, 2), pieces, (0, 0, 0, 0, 2)):
        for dy in range(base, base + piece.shape[0] // (2 * SHARD)):
            from_x, from_y = (x + 4 - dx) % 4, (y + 4 - dy) % 4
            for side in range(2):
                from_zh = zh if side == 0 else 1 - zh
                slot = (from_zh * 4 + from_x) ^ head
                row = pl.multiple_of((slot * 4 + from_y) * SHARD, SHARD)
                at = (2 * (dy - base) + side) * SHARD
                weights[pl.ds(row, SHARD), :] = piece[at : at + SHARD, :]
    rates[...] = jnp.zeros_like(rates)
    for slot in range(8):
        source = pl.multiple_of((slot ^ head) * BLOCK, BLOCK)
        rates[:1, slot * BLOCK : (slot + 1) * BLOCK] = rate[:, pl.ds(source, BLOCK)]
    load_tokens(blocks, 0, tokens)
    finish_projection(
        tokens[...], weights[...], rates[...], queries, keys_grads, values_wide
    )


def project_second(begins, weights, rates, *refs):
    blocks = refs[:8]
    queries, keys_grads, values_wide, tokens = refs[8:]
    load_tokens(blocks, SPAN, tokens)
    finish_projection(
        tokens[...], weights[...], rates[...], queries, keys_grads, values_wide
    )


def soft_weights(scores, keep=None):
    soft = jnp.exp2(scores * (LOG2E / SCORE) - SCORE * LOG2E)
    if keep is not None:
        soft = jnp.where(keep, soft, 0.0)
    return soft.astype(BF)


def corner(row0, own):
    a = lax.broadcasted_iota(jnp.int32, (256, SPAN), 0) + row0
    j = lax.broadcasted_iota(jnp.int32, (256, SPAN), 1)
    return j <= a if own else j > a


def attend_past(q, row0, keys, values, first):
    total = None
    for at in range(first, WINDOW, SPAN):
        cols = slice(at, at + SPAN)
        keep = corner(row0, False) if at == first else None
        part = matmul_nt(soft_weights(matmul(q, keys[:, cols]), keep), values[:, cols])
        total = part if total is None else total + part
    return total


def attend_own(q, row0, keys, values, causal):
    keep = corner(row0, True) if causal else None
    return matmul(soft_weights(matmul_nt(q, keys), keep), values)


def fast_read(q, weights):
    total = None
    for at in range(0, HID, 256):
        gate = matmul(q, weights(at)) * (1.0 / SCORE)
        lift = matmul(q, weights(HID + at)) * (1.0 / SCORE)
        hidden = (gate * sigmoid(gate) * lift).astype(BF)
        part = matmul_nt(hidden, weights(2 * HID + at))
        total = part if total is None else total + part
    return total * (1.0 / ROOT_HID)


def fast_write(keys_grads, weights, momentum, weights_out, momentum_out):
    y = keys_grads[:, :HD]
    g = keys_grads[:, HD:]
    y_turned = y.astype(F32).T.astype(BF)
    g_turned = g.astype(F32).T.astype(BF)
    for at in range(0, HID, 256):
        spots = (at, HID + at, 2 * HID + at)
        now = [weights(spot) for spot in spots]
        u1, u3, p = (w.astype(BF) for w in now)
        gate = matmul(y, u1) * (1.0 / SCORE)
        lift = matmul(y, u3) * (1.0 / SCORE)
        err = matmul(g, p) * (1.0 / ROOT_HID)
        sg = sigmoid(gate)
        silu = gate * sg
        gate_grad = (err * lift * sg * (1.0 + gate * (1.0 - sg))).astype(BF)
        lift_grad = (err * silu).astype(BF)
        hidden = (silu * lift).astype(BF)
        grads = (
            matmul(y_turned, gate_grad) * (1.0 / SCORE),
            matmul(y_turned, lift_grad) * (1.0 / SCORE),
            matmul(g_turned, hidden) * (1.0 / ROOT_HID),
        )
        for spot, w, grad in zip(spots, now, grads):
            m = 0.9 * momentum(spot) + grad
            stepped = w - m
            scale = lax.rsqrt(jnp.mean(stepped * stepped, axis=0, keepdims=True) + EPS)
            weights_out(spot, stepped * scale)
            momentum_out(spot, m)


def first_mix(begins, queries, keys_grads, values, past_keys, past_values, fast_far, initial_far, done, mix, fast, initial, arrived):
    copies = [
        pltpu.make_async_copy(fast_far, fast, arrived.at[0]),
        pltpu.make_async_copy(initial_far, initial, arrived.at[1]),
    ]
    for copy in copies:
        copy.start()
    fresh = begins[0, lax.axis_index(SEQ)] > 0
    seen = jnp.where(fresh, 0.0, 1.0)
    for row in range(0, SPAN, 256):
        q = queries[row : row + 256, :]
        past = attend_past(q, row, past_keys, past_values, 0)
        own = attend_own(q, row, keys_grads[:, :HD], values[...], True)
        total = past * seen + own
        attended = total[:, :HD] / total[:, HD : HD + 1]
        if row == 0:
            for copy in copies:
                copy.wait()
        applied = fast_read(
            q,
            lambda at: jnp.where(
                fresh, initial[:, at : at + 256].astype(F32), fast[:, at : at + 256]
            ).astype(BF),
        )
        mix[:, row : row + 256] = (attended + applied).T.astype(BF)


def lend_window(begins, queries, past_keys, past_values, keys_grads, values, mix, part):
    seq = lax.axis_index(SEQ)
    old = jnp.where(begins[0, seq] > 0, 0.0, 1.0)
    seen = jnp.where(begins[1, (seq + 1) % 32] > 0, 0.0, 1.0)
    for row in range(0, SPAN, 256):
        q = queries[row : row + 256, :]
        past = attend_past(q, row, past_keys, past_values, SPAN)
        new = attend_own(q, row, keys_grads[:, :HD], values[...], False)
        total = (past * old + new) * seen
        weight = total[:, HD : HD + 1]
        high = weight.astype(BF).astype(F32)
        lane = lax.broadcasted_iota(jnp.int32, (256, 64), 1)
        tail = jnp.where(lane == 0, high, jnp.where(lane == 1, weight - high, 0.0))
        part[row : row + 256, :] = jnp.concatenate([total[:, :HD], tail], axis=1).astype(BF)


def arrive_state(begins, keys_grads, state, initial, fast_out, momentum_out):
    seq = lax.axis_index(SEQ)
    fresh_before = begins[0, (seq + 31) % 32] > 0
    fresh = begins[1, seq] > 0

    def rows_of(first, at):
        return jnp.concatenate(
            [state[first + b, :, at : at + 256].astype(F32) for b in range(8)], axis=0
        )

    def weights(at):
        return jnp.where(
            fresh_before,
            initial[:, at : at + 256].astype(F32),
            rows_of(0, at),
        )

    def moment(at):
        return jnp.where(fresh_before, 0.0, rows_of(8, at))

    def keep_weights(at, value):
        fast_out[:, at : at + 256] = jnp.where(
            fresh, initial[:, at : at + 256].astype(F32), value
        )

    def keep_moment(at, value):
        momentum_out[:, at : at + 256] = jnp.where(fresh, 0.0, value)

    fast_write(keys_grads, weights, moment, keep_weights, keep_moment)


def second_mix(begins, queries, keys_grads, values, fast, part, mix):
    for row in range(0, SPAN, 256):
        rows = slice(row, row + 256)
        q = queries[rows, :]
        total = attend_own(q, row, keys_grads[:, :HD], values[...], True)
        lent = part[rows, :].astype(F32)
        weight = total[:, HD : HD + 1] + lent[:, HD : HD + 1] + lent[:, HD + 1 : HD + 2]
        attended = (total[:, :HD] + lent[:, :HD]) / weight
        applied = fast_read(q, lambda at: fast[:, at : at + 256].astype(BF))
        mix[:, rows] = (attended + applied).T.astype(BF)


def last_state(
    begins, keys_grads, fast, momentum, fast_far, momentum_far, fast_out, momentum_out, sent
):
    def keep_weights(at, value):
        fast_out[:, at : at + 256] = value

    def keep_moment(at, value):
        momentum_out[:, at : at + 256] = value

    fast_write(
        keys_grads,
        lambda at: fast[:, at : at + 256],
        lambda at: momentum[:, at : at + 256],
        keep_weights,
        keep_moment,
    )
    copies = [
        pltpu.make_async_copy(fast_out, fast_far, sent.at[0]),
        pltpu.make_async_copy(momentum_out, momentum_far, sent.at[1]),
    ]
    for copy in copies:
        copy.start()
    for copy in copies:
        copy.wait()


def matmul_tn(a, b):
    return lax.dot_general(a, b, (((0,), (0,)), ((), ())), preferred_element_type=F32)


def project_mix(own, near, got, near_got, mine, theirs):
    total = matmul_tn(own[...], mine[:HD, :]) + matmul_tn(near[...], theirs[:HD, :])
    for k in (1, 2, 3):
        rows = slice(k * HD, (k + 1) * HD)
        total = total + matmul_tn(got[k - 1], mine[rows, :])
        total = total + matmul_tn(near_got[k - 1], theirs[rows, :])
    return total.astype(BF)


def project_out_first(begins, own, near, got, near_got, mine, theirs, done, out):
    out[...] = project_mix(own, near, got, near_got, mine, theirs)


def project_out_last(begins, own, near, got, near_got, mine, theirs, earlier, out):
    out[:SPAN, :] = earlier[...]
    out[SPAN:, :] = project_mix(own, near, got, near_got, mine, theirs)


def body(
    tokens,
    fast_state,
    momentum,
    init_fast,
    past_keys,
    past_values,
    qkv_weight,
    rate_weight,
    out_weight,
    prompt_begins,
):
    seq = lax.axis_index(SEQ)
    shard = call(build_shard, shape(SHARD, WIDE), prompt_begins, qkv_weight)
    across = move(shard, ZH)
    pair = call(join, shape(2 * SHARD, WIDE), prompt_begins, shard, across)
    token_rows = call(
        copy_rows, shape(2 * SPAN, BLOCK), prompt_begins, tokens[0], across, after=1
    )
    column = call(
        join,
        shape(8 * SHARD, WIDE),
        prompt_begins,
        pair,
        *[move(pair, YS[k]) for k in (1, 2, 3)],
    )
    left = move(column, XS[1])
    right = move(column, XS[3])
    pieces = [column, left, right, move(left[:384], XS[1]), move(right[384:], XS[3])]
    all_tokens = gather_tokens(token_rows)
    state = call(
        pack_state,
        shape(16, 24, 3 * HID),
        prompt_begins,
        fast_state[0, 0],
        momentum[0, 0],
    )
    shares = lax.all_to_all(state, "xy", 0, 0, tiled=False)
    shares = call(
        turn,
        shape(16, 24, 3 * HID),
        prompt_begins,
        shares,
        move(shares[15], ZH),
        left,
        right,
        after=2,
    )
    state_sent = lax.all_to_all(shares, "xy", 0, 0, tiled=False)
    out_parts = call(
        split_out,
        tuple(shape(HD, 2 * BLOCK) for _ in range(4)),
        prompt_begins,
        out_weight,
        all_tokens[6],
        pieces[3],
        pieces[4],
        after=3,
    )
    out_parts = [out_parts[0]] + [
        move(part, route) for part, route in zip(out_parts[1:], (ZL1, ZL2, ZL3))
    ]
    unit_keys, wide_values = call(
        prepare_window,
        (shape(HD, WINDOW), shape(256, WINDOW)),
        prompt_begins,
        past_keys[0].T,
        past_values[0].T,
        moved=4 << 20,
    )
    span_outs = (shape(SPAN, HD), shape(SPAN, 2 * HD), shape(SPAN, 256))
    token_room = pltpu.VMEM((SPAN, 8 * BLOCK), BF)
    weights, rates, q0, kg0, v0 = call(
        project_first,
        (shape(8 * BLOCK, WIDE), shape(16, 8 * BLOCK)) + span_outs,
        prompt_begins,
        rate_weight.T,
        *all_tokens,
        *pieces,
        flops=2 * SPAN * 3072 * WIDE,
        moved=12 << 20,
        scratch=[token_room],
    )
    kg_before = move(kg0, FORWARD)
    mix0 = call(
        first_mix,
        shape(HD, SPAN),
        prompt_begins,
        q0,
        kg0,
        v0,
        unit_keys,
        wide_values,
        fast_state[0, 0],
        init_fast[0],
        state_sent,
        flops=4 << 30,
        moved=6 << 20,
        after=3,
        scratch=[
            pltpu.VMEM((HD, 3 * HID), F32),
            pltpu.VMEM((HD, 3 * HID), BF),
            pltpu.SemaphoreType.DMA((2,)),
        ],
    )

    q1, kg1, v1 = call(
        project_second,
        span_outs,
        prompt_begins,
        weights,
        rates,
        *all_tokens,
        flops=2 * SPAN * 3072 * WIDE,
        moved=8 << 20,
        scratch=[token_room],
    )
    q_next = move(q1, BACK)
    part = call(
        lend_window,
        shape(SPAN, 256),
        prompt_begins,
        q_next,
        unit_keys,
        wide_values,
        kg0,
        v0,
        mix0,
        flops=3 << 30,
        moved=3 << 20,
        after=1,
    )
    part_before = move(part, FORWARD)
    state = shape(HD, 3 * HID, dtype=F32)
    fast1, momentum1 = call(
        arrive_state,
        (state, state),
        prompt_begins,
        kg_before,
        state_sent,
        init_fast[0],
        flops=3 << 30,
        moved=6 << 20,
    )
    out_mine, out_theirs = call(
        sort_out,
        (shape(4 * HD, BLOCK), shape(4 * HD, BLOCK)),
        prompt_begins,
        *out_parts,
        fast1,
        after=1,
    )
    out_rows = (out_mine, move(out_theirs, CORE))

    def gather_mix(mix, done):
        near = move(mix, CORE)
        got = call(
            collect,
            shape(3, HD, SPAN),
            prompt_begins,
            *[move(mix, route) for route in (ZL1, ZL2, ZL3)],
            done,
            after=1,
        )
        return (mix, near, got, move(got, CORE)) + out_rows

    cost = dict(flops=2 * SPAN * 1536 * BLOCK, moved=4 << 20)
    mix1 = call(
        second_mix,
        shape(HD, SPAN),
        prompt_begins,
        q1,
        kg1,
        v1,
        fast1,
        part_before,
        flops=2 << 30,
        moved=3 << 20,
    )
    fast2, momentum2 = call(
        last_state,
        (state, state),
        prompt_begins,
        kg1,
        fast1,
        momentum1,
        flops=3 << 30,
        moved=8 << 20,
        place=ANY,
        scratch=[
            pltpu.VMEM((HD, 3 * HID), F32),
            pltpu.VMEM((HD, 3 * HID), F32),
            pltpu.SemaphoreType.DMA((2,)),
        ],
    )
    mix0_all = gather_mix(mix0, fast1)
    out0 = call(
        project_out_first,
        shape(SPAN, BLOCK),
        prompt_begins,
        *mix0_all,
        mix1,
        after=1,
        **cost,
    )
    mix1_all = gather_mix(mix1, fast2)
    mixed = call(
        project_out_last, shape(2 * SPAN, BLOCK), prompt_begins, *mix1_all, out0, **cost
    )
    return mixed[None], fast2[None, None], momentum2[None, None]


def solution(mesh):
    in_specs = (
        P(SEQ, None, "head"),
        P(SEQ, "head", None, None),
        P(SEQ, "head", None, None),
        P("head", None, None),
        P(SEQ, None, "head"),
        P(SEQ, None, "head"),
        P(None, SEQ, "head"),
        P(None, "head"),
        P("head", None),
        P(),
    )
    out_specs = (P(SEQ, None, "head"), P(SEQ, "head", None, None), P(SEQ, "head", None, None))
    mesh = Mesh(mesh.devices.reshape(2, 16, 8), AXES)
    return jax.shard_map(body, mesh=mesh, in_specs=in_specs, out_specs=out_specs, check_vma=False)
```

```python
import math

import jax
import jax.numpy as jnp
from jax import lax
from jax.experimental import pallas as pl
from jax.experimental.pallas import tpu as pltpu
from jax.sharding import Mesh, PartitionSpec as P

SPAN = 512
WINDOW = 2048
HD = 192
HID = 768
SHARD = 96
WIDE = 640
BLOCK = 384
SEQ = ("zh", "xy")
AXES = ("zh", "xy", "head")
EPS = 1e-06
LOG2E = 1.4426950408889634
SCORE = math.sqrt(HD)
ROOT_HID = math.sqrt(HID)
BF = jnp.bfloat16
F32 = jnp.float32
VMEM = pl.BlockSpec(memory_space=pltpu.VMEM)
SMEM = pl.BlockSpec(memory_space=pltpu.SMEM)
ANY = pl.BlockSpec(memory_space=pl.ANY)


def pairs(target):
    out = []
    for i in range(256):
        s, h = i // 8, i % 8
        goal = target(s // 16, (s // 4) % 4, s % 4, h // 2, h % 2)
        if goal is not None:
            zh, x, y, zl, c = goal
            out.append((i, ((zh * 4 + x) * 4 + y) * 8 + zl * 2 + c))
    return out


def step_pairs(distance):
    return [(i, ((i // 8 + distance) % 32) * 8 + i % 8) for i in range(256)]


CORE = pairs(lambda zh, x, y, zl, c: (zh, x, y, zl, 1 - c))
ZL1 = pairs(lambda zh, x, y, zl, c: (zh, x, y, zl ^ 1, c))
ZL2 = pairs(lambda zh, x, y, zl, c: (zh, x, y, zl ^ 2, c))
ZL3 = pairs(lambda zh, x, y, zl, c: (zh, x, y, zl ^ 3, c))
ZH = pairs(lambda zh, x, y, zl, c: (1 - zh, x, y, zl, c))
XS = [pairs(lambda zh, x, y, zl, c, k=k: (zh, (x + k) % 4, y, zl, c)) for k in range(4)]
YS = [pairs(lambda zh, x, y, zl, c, k=k: (zh, x, (y + k) % 4, zl, c)) for k in range(4)]
FORWARD = step_pairs(1)
BACK = step_pairs(-1)


def move(array, route):
    return lax.ppermute(array, AXES, route)


def gather_tokens(block):
    near = move(block, CORE)
    one = move(block, ZL1)
    two = move(block, ZL2)
    three = move(two, ZL1)
    return [block, near, one, move(one, CORE), two, move(two, CORE), three, move(three, CORE)]


def matmul(a, b):
    return jnp.dot(a, b, preferred_element_type=F32)


def matmul_nt(a, b):
    return lax.dot_general(a, b, (((1,), (1,)), ((), ())), preferred_element_type=F32)


def unit(rows):
    return rows * lax.rsqrt(jnp.mean(rows * rows, axis=-1, keepdims=True) + EPS)


def sigmoid(a):
    return 1.0 / (1.0 + jnp.exp(-a))


def with_ones(values):
    rows = values.shape[0]
    lane = lax.broadcasted_iota(jnp.int32, (rows, 64), 1)
    return jnp.concatenate([values.astype(F32), jnp.where(lane == 0, 1.0, 0.0)], axis=1).astype(BF)


def call(kernel, outs, *args, flops=0, moved=0, scratch=(), limit=40, after=0, place=VMEM):
    return pl.pallas_call(
        kernel,
        out_shape=outs,
        in_specs=[SMEM] + [VMEM] * (len(args) - 1 - after) + [ANY] * after,
        out_specs=jax.tree.map(lambda _: place, outs),
        scratch_shapes=list(scratch),
        compiler_params=pltpu.CompilerParams(vmem_limit_bytes=limit * 1024 * 1024),
        cost_estimate=pl.CostEstimate(flops=flops, bytes_accessed=moved, transcendentals=0),
    )(*args)


def shape(*dims, dtype=BF):
    return jax.ShapeDtypeStruct(dims, dtype)


def prepare_window(begins, keys, values, unit_keys, wide_values):
    k = keys[...].astype(F32)
    unit_keys[...] = (k * lax.rsqrt(jnp.mean(k * k, axis=0, keepdims=True) + EPS)).astype(BF)
    wide_values[:HD, :] = values[...]
    row = lax.broadcasted_iota(jnp.int32, (64, WINDOW), 0)
    wide_values[HD:, :] = jnp.where(row == 0, 1.0, 0.0).astype(BF)


def build_shard(begins, weight, out):
    for c in range(3):
        out[:, c * HD : (c + 1) * HD] = weight[c]
    out[:, 3 * HD :] = jnp.zeros((SHARD, WIDE - 3 * HD), BF)


def join(begins, *refs):
    out = refs[-1]
    rows = refs[0].shape[0]
    for b, ref in enumerate(refs[:-1]):
        out[b * rows : (b + 1) * rows, :] = ref[...]


def join_column(begins, *refs):
    join(begins, *refs[:4], refs[-1])


def copy_rows(begins, rows, done, first, second):
    first[...] = rows[:SPAN, :]
    second[...] = rows[SPAN:, :]


def pack_state(begins, fast, momentum, done, out):
    for b in range(8):
        out[b] = fast[24 * b : 24 * (b + 1), :].astype(BF)
        out[8 + b] = momentum[24 * b : 24 * (b + 1), :].astype(BF)


def turn(begins, shares, other, done, done_too, out):
    out[0] = other[...]
    for b in range(15):
        out[b + 1] = shares[b]


def split_out(begins, weight, *refs):
    outs = refs[1:]
    zl = lax.axis_index("head") // 2
    for k in range(4):
        at = pl.multiple_of((zl ^ k) * 2 * BLOCK, 2 * BLOCK)
        outs[k][...] = weight[:, pl.ds(at, 2 * BLOCK)]


def sort_out(begins, *refs):
    mine, theirs = refs[5:]
    core = lax.axis_index("head") % 2
    for k in range(4):
        rows = slice(k * HD, (k + 1) * HD)
        for out, side in ((mine, core), (theirs, 1 - core)):
            out[rows, :] = refs[k][:, pl.ds(pl.multiple_of(side * BLOCK, BLOCK), BLOCK)]


def collect(begins, one, two, three, done, out):
    out[0] = one[...]
    out[1] = two[...]
    out[2] = three[...]


def finish_projection(tokens, weights, rates, queries, keys_grads, values_wide):
    product = matmul(tokens, weights)
    rate = matmul_nt(tokens, rates)[:, :1]
    q = product[:, :HD].astype(BF).astype(F32)
    k = product[:, HD : 2 * HD].astype(BF).astype(F32)
    v = product[:, 2 * HD : 3 * HD].astype(BF)
    soft = jnp.maximum(rate, 0.0) + jnp.log(1.0 + jnp.exp(-jnp.abs(rate)))
    step = (0.3 * soft).astype(BF).astype(F32)
    grad = -step * v.astype(F32)
    queries[...] = unit(q).astype(BF)
    keys_grads[...] = jnp.concatenate([unit(k), grad], axis=1).astype(BF)
    values_wide[...] = with_ones(v)


def load_tokens(blocks, tokens):
    for b, block in enumerate(blocks):
        tokens[:, b * BLOCK : (b + 1) * BLOCK] = block[...]


def project_first(begins, rate, *refs):
    blocks = refs[:8]
    pieces = refs[8:13]
    weights, rates, queries, keys_grads, values_wide, tokens = refs[13:]
    seq, head = lax.axis_index(SEQ), lax.axis_index("head")
    zh, x, y = seq // 16, (seq // 4) % 4, seq % 4
    for dx, piece, base in zip((0, 1, 3, 2, 2), pieces, (0, 0, 0, 0, 2)):
        for dy in range(base, base + piece.shape[0] // (2 * SHARD)):
            from_x, from_y = (x + 4 - dx) % 4, (y + 4 - dy) % 4
            for side in range(2):
                from_zh = zh if side == 0 else 1 - zh
                slot = (from_zh * 4 + from_x) ^ head
                row = pl.multiple_of((slot * 4 + from_y) * SHARD, SHARD)
                at = (2 * (dy - base) + side) * SHARD
                weights[pl.ds(row, SHARD), :] = piece[at : at + SHARD, :]
    rates[...] = jnp.zeros_like(rates)
    for slot in range(8):
        source = pl.multiple_of((slot ^ head) * BLOCK, BLOCK)
        rates[:1, slot * BLOCK : (slot + 1) * BLOCK] = rate[:, pl.ds(source, BLOCK)]
    load_tokens(blocks, tokens)
    finish_projection(
        tokens[...], weights[...], rates[...], queries, keys_grads, values_wide
    )


def project_second(begins, weights, rates, *refs):
    blocks = refs[:8]
    queries, keys_grads, values_wide, tokens = refs[8:]
    load_tokens(blocks, tokens)
    finish_projection(
        tokens[...], weights[...], rates[...], queries, keys_grads, values_wide
    )


def soft_weights(scores, keep=None):
    soft = jnp.exp2(scores * (LOG2E / SCORE) - SCORE * LOG2E)
    if keep is not None:
        soft = jnp.where(keep, soft, 0.0)
    return soft.astype(BF)


def corner(row0, own):
    a = lax.broadcasted_iota(jnp.int32, (256, SPAN), 0) + row0
    j = lax.broadcasted_iota(jnp.int32, (256, SPAN), 1)
    return j <= a if own else j > a


def attend_past(q, row0, keys, values, first):
    total = None
    for at in range(first, WINDOW, SPAN):
        cols = slice(at, at + SPAN)
        keep = corner(row0, False) if at == first else None
        part = matmul_nt(soft_weights(matmul(q, keys[:, cols]), keep), values[:, cols])
        total = part if total is None else total + part
    return total


def attend_own(q, row0, keys, values, causal):
    keep = corner(row0, True) if causal else None
    return matmul(soft_weights(matmul_nt(q, keys), keep), values)


def fast_read(q, weights):
    total = None
    for at in range(0, HID, 256):
        gate = matmul(q, weights(at)) * (1.0 / SCORE)
        lift = matmul(q, weights(HID + at)) * (1.0 / SCORE)
        hidden = (gate * sigmoid(gate) * lift).astype(BF)
        part = matmul_nt(hidden, weights(2 * HID + at))
        total = part if total is None else total + part
    return total * (1.0 / ROOT_HID)


def fast_write(keys_grads, weights, momentum, weights_out, momentum_out):
    y = keys_grads[:, :HD]
    g = keys_grads[:, HD:]
    y_turned = y.astype(F32).T.astype(BF)
    g_turned = g.astype(F32).T.astype(BF)
    for at in range(0, HID, 256):
        spots = (at, HID + at, 2 * HID + at)
        now = [weights(spot) for spot in spots]
        u1, u3, p = (w.astype(BF) for w in now)
        gate = matmul(y, u1) * (1.0 / SCORE)
        lift = matmul(y, u3) * (1.0 / SCORE)
        err = matmul(g, p) * (1.0 / ROOT_HID)
        sg = sigmoid(gate)
        silu = gate * sg
        gate_grad = (err * lift * sg * (1.0 + gate * (1.0 - sg))).astype(BF)
        lift_grad = (err * silu).astype(BF)
        hidden = (silu * lift).astype(BF)
        grads = (
            matmul(y_turned, gate_grad) * (1.0 / SCORE),
            matmul(y_turned, lift_grad) * (1.0 / SCORE),
            matmul(g_turned, hidden) * (1.0 / ROOT_HID),
        )
        for spot, w, grad in zip(spots, now, grads):
            m = 0.9 * momentum(spot) + grad
            stepped = w - m
            scale = lax.rsqrt(jnp.mean(stepped * stepped, axis=0, keepdims=True) + EPS)
            weights_out(spot, stepped * scale)
            momentum_out(spot, m)


def first_mix(begins, queries, keys_grads, values, past_keys, past_values, fast_far, initial_far, mix, fast, initial, arrived):
    copies = [
        pltpu.make_async_copy(fast_far, fast, arrived.at[0]),
        pltpu.make_async_copy(initial_far, initial, arrived.at[1]),
    ]
    for copy in copies:
        copy.start()
    fresh = begins[0, lax.axis_index(SEQ)] > 0
    seen = jnp.where(fresh, 0.0, 1.0)
    for row in range(0, SPAN, 256):
        q = queries[row : row + 256, :]
        past = attend_past(q, row, past_keys, past_values, 0)
        own = attend_own(q, row, keys_grads[:, :HD], values[...], True)
        total = past * seen + own
        attended = total[:, :HD] / total[:, HD : HD + 1]
        if row == 0:
            for copy in copies:
                copy.wait()
        applied = fast_read(
            q,
            lambda at: jnp.where(
                fresh, initial[:, at : at + 256].astype(F32), fast[:, at : at + 256]
            ).astype(BF),
        )
        mix[:, row : row + 256] = (attended + applied).T.astype(BF)


def lend_window(begins, queries, past_keys, past_values, keys_grads, values, mix, part):
    seq = lax.axis_index(SEQ)
    old = jnp.where(begins[0, seq] > 0, 0.0, 1.0)
    seen = jnp.where(begins[1, (seq + 1) % 32] > 0, 0.0, 1.0)
    for row in range(0, SPAN, 256):
        q = queries[row : row + 256, :]
        past = attend_past(q, row, past_keys, past_values, SPAN)
        new = attend_own(q, row, keys_grads[:, :HD], values[...], False)
        total = (past * old + new) * seen
        weight = total[:, HD : HD + 1]
        high = weight.astype(BF).astype(F32)
        lane = lax.broadcasted_iota(jnp.int32, (256, 64), 1)
        tail = jnp.where(lane == 0, high, jnp.where(lane == 1, weight - high, 0.0))
        part[row : row + 256, :] = jnp.concatenate([total[:, :HD], tail], axis=1).astype(BF)


def arrive_state(begins, keys_grads, state, initial, done, fast_out, momentum_out):
    seq = lax.axis_index(SEQ)
    fresh_before = begins[0, (seq + 31) % 32] > 0
    fresh = begins[1, seq] > 0

    def rows_of(first, at):
        return jnp.concatenate(
            [state[first + b, :, at : at + 256].astype(F32) for b in range(8)], axis=0
        )

    def weights(at):
        return jnp.where(
            fresh_before,
            initial[:, at : at + 256].astype(F32),
            rows_of(0, at),
        )

    def moment(at):
        return jnp.where(fresh_before, 0.0, rows_of(8, at))

    def keep_weights(at, value):
        fast_out[:, at : at + 256] = jnp.where(
            fresh, initial[:, at : at + 256].astype(F32), value
        )

    def keep_moment(at, value):
        momentum_out[:, at : at + 256] = jnp.where(fresh, 0.0, value)

    fast_write(keys_grads, weights, moment, keep_weights, keep_moment)


def second_mix(begins, queries, keys_grads, values, fast, part, mix):
    for row in range(0, SPAN, 256):
        rows = slice(row, row + 256)
        q = queries[rows, :]
        total = attend_own(q, row, keys_grads[:, :HD], values[...], True)
        lent = part[rows, :].astype(F32)
        weight = total[:, HD : HD + 1] + lent[:, HD : HD + 1] + lent[:, HD + 1 : HD + 2]
        attended = (total[:, :HD] + lent[:, :HD]) / weight
        applied = fast_read(q, lambda at: fast[:, at : at + 256].astype(BF))
        mix[:, rows] = (attended + applied).T.astype(BF)


def last_state(
    begins, keys_grads, fast, momentum, fast_far, momentum_far, fast_out, momentum_out, sent
):
    def keep_weights(at, value):
        fast_out[:, at : at + 256] = value

    def keep_moment(at, value):
        momentum_out[:, at : at + 256] = value

    fast_write(
        keys_grads,
        lambda at: fast[:, at : at + 256],
        lambda at: momentum[:, at : at + 256],
        keep_weights,
        keep_moment,
    )
    copies = [
        pltpu.make_async_copy(fast_out, fast_far, sent.at[0]),
        pltpu.make_async_copy(momentum_out, momentum_far, sent.at[1]),
    ]
    for copy in copies:
        copy.start()
    for copy in copies:
        copy.wait()


def matmul_tn(a, b):
    return lax.dot_general(a, b, (((0,), (0,)), ((), ())), preferred_element_type=F32)


def project_mix(own, near, got, near_got, mine, theirs):
    total = matmul_tn(own[...], mine[:HD, :]) + matmul_tn(near[...], theirs[:HD, :])
    for k in (1, 2, 3):
        rows = slice(k * HD, (k + 1) * HD)
        total = total + matmul_tn(got[k - 1], mine[rows, :])
        total = total + matmul_tn(near_got[k - 1], theirs[rows, :])
    return total.astype(BF)


def project_out_first(begins, own, near, got, near_got, mine, theirs, done, out):
    out[...] = project_mix(own, near, got, near_got, mine, theirs)


def project_out_last(begins, own, near, got, near_got, mine, theirs, earlier, out):
    out[:SPAN, :] = earlier[...]
    out[SPAN:, :] = project_mix(own, near, got, near_got, mine, theirs)


def body(
    tokens,
    fast_state,
    momentum,
    init_fast,
    past_keys,
    past_values,
    qkv_weight,
    rate_weight,
    out_weight,
    prompt_begins,
):
    seq = lax.axis_index(SEQ)
    shard = call(build_shard, shape(SHARD, WIDE), prompt_begins, qkv_weight)
    across = move(shard, ZH)
    pair = call(join, shape(2 * SHARD, WIDE), prompt_begins, shard, across)
    token_rows = call(
        copy_rows,
        (shape(SPAN, BLOCK), shape(SPAN, BLOCK)),
        prompt_begins,
        tokens[0],
        across,
        after=1,
    )
    first_tokens, second_tokens = (gather_tokens(rows) for rows in token_rows)
    column = call(
        join_column,
        shape(8 * SHARD, WIDE),
        prompt_begins,
        pair,
        *[move(pair, YS[k]) for k in (1, 2, 3)],
        first_tokens[2],
        first_tokens[4],
        after=2,
    )
    left = move(column, XS[1])
    right = move(column, XS[3])
    pieces = [column, left, right, move(left[:384], XS[1]), move(right[384:], XS[3])]
    state = call(
        pack_state,
        shape(16, 24, 3 * HID),
        prompt_begins,
        fast_state[0, 0],
        momentum[0, 0],
        column,
        after=1,
    )
    shares = lax.all_to_all(state, "xy", 0, 0, tiled=False)
    shares = call(
        turn,
        shape(16, 24, 3 * HID),
        prompt_begins,
        shares,
        move(shares[15], ZH),
        pieces[3],
        pieces[4],
        after=2,
    )
    state_sent = lax.all_to_all(shares, "xy", 0, 0, tiled=False)
    unit_keys, wide_values = call(
        prepare_window,
        (shape(HD, WINDOW), shape(256, WINDOW)),
        prompt_begins,
        past_keys[0].T,
        past_values[0].T,
        moved=4 << 20,
    )
    span_outs = (shape(SPAN, HD), shape(SPAN, 2 * HD), shape(SPAN, 256))
    token_room = pltpu.VMEM((SPAN, 8 * BLOCK), BF)
    weights, rates, q0, kg0, v0 = call(
        project_first,
        (shape(8 * BLOCK, WIDE), shape(16, 8 * BLOCK)) + span_outs,
        prompt_begins,
        rate_weight.T,
        *first_tokens,
        *pieces,
        flops=2 * SPAN * 3072 * WIDE,
        moved=12 << 20,
        scratch=[token_room],
    )
    kg_before = move(kg0, FORWARD)
    out_parts = call(
        split_out,
        tuple(shape(HD, 2 * BLOCK) for _ in range(4)),
        prompt_begins,
        out_weight,
        q0,
        after=1,
    )
    out_parts = [out_parts[0]] + [
        move(part, route) for part, route in zip(out_parts[1:], (ZL1, ZL2, ZL3))
    ]
    mix0 = call(
        first_mix,
        shape(HD, SPAN),
        prompt_begins,
        q0,
        kg0,
        v0,
        unit_keys,
        wide_values,
        fast_state[0, 0],
        init_fast[0],
        flops=4 << 30,
        moved=6 << 20,
        after=2,
        scratch=[
            pltpu.VMEM((HD, 3 * HID), F32),
            pltpu.VMEM((HD, 3 * HID), BF),
            pltpu.SemaphoreType.DMA((2,)),
        ],
    )

    q1, kg1, v1 = call(
        project_second,
        span_outs,
        prompt_begins,
        weights,
        rates,
        *second_tokens,
        flops=2 * SPAN * 3072 * WIDE,
        moved=8 << 20,
        scratch=[token_room],
    )
    q_next = move(q1, BACK)
    part = call(
        lend_window,
        shape(SPAN, 256),
        prompt_begins,
        q_next,
        unit_keys,
        wide_values,
        kg0,
        v0,
        mix0,
        flops=3 << 30,
        moved=3 << 20,
        after=1,
    )
    part_before = move(part, FORWARD)
    out_mine, out_theirs = call(
        sort_out,
        (shape(4 * HD, BLOCK), shape(4 * HD, BLOCK)),
        prompt_begins,
        *out_parts,
        part,
        after=1,
    )
    out_rows = (out_mine, move(out_theirs, CORE))
    state = shape(HD, 3 * HID, dtype=F32)
    fast1, momentum1 = call(
        arrive_state,
        (state, state),
        prompt_begins,
        kg_before,
        state_sent,
        init_fast[0],
        out_mine,
        after=1,
        flops=3 << 30,
        moved=6 << 20,
    )
    def gather_mix(mix, done):
        near = move(mix, CORE)
        got = call(
            collect,
            shape(3, HD, SPAN),
            prompt_begins,
            *[move(mix, route) for route in (ZL1, ZL2, ZL3)],
            done,
            after=1,
        )
        return (mix, near, got, move(got, CORE)) + out_rows

    cost = dict(flops=2 * SPAN * 1536 * BLOCK, moved=4 << 20)
    mix1 = call(
        second_mix,
        shape(HD, SPAN),
        prompt_begins,
        q1,
        kg1,
        v1,
        fast1,
        part_before,
        flops=2 << 30,
        moved=3 << 20,
    )
    fast2, momentum2 = call(
        last_state,
        (state, state),
        prompt_begins,
        kg1,
        fast1,
        momentum1,
        flops=3 << 30,
        moved=8 << 20,
        place=ANY,
        scratch=[
            pltpu.VMEM((HD, 3 * HID), F32),
            pltpu.VMEM((HD, 3 * HID), F32),
            pltpu.SemaphoreType.DMA((2,)),
        ],
    )
    mix0_all = gather_mix(mix0, fast1)
    out0 = call(
        project_out_first,
        shape(SPAN, BLOCK),
        prompt_begins,
        *mix0_all,
        mix1,
        after=1,
        **cost,
    )
    mix1_all = gather_mix(mix1, fast2)
    mixed = call(
        project_out_last, shape(2 * SPAN, BLOCK), prompt_begins, *mix1_all, out0, **cost
    )
    return mixed[None], fast2[None, None], momentum2[None, None]


def solution(mesh):
    in_specs = (
        P(SEQ, None, "head"),
        P(SEQ, "head", None, None),
        P(SEQ, "head", None, None),
        P("head", None, None),
        P(SEQ, None, "head"),
        P(SEQ, None, "head"),
        P(None, SEQ, "head"),
        P(None, "head"),
        P("head", None),
        P(),
    )
    out_specs = (P(SEQ, None, "head"), P(SEQ, "head", None, None), P(SEQ, "head", None, None))
    mesh = Mesh(mesh.devices.reshape(2, 16, 8), AXES)
    return jax.shard_map(body, mesh=mesh, in_specs=in_specs, out_specs=out_specs, check_vma=False)
```

```python
import math

import jax
import jax.numpy as jnp
from jax import lax
from jax.experimental import pallas as pl
from jax.experimental.pallas import tpu as pltpu
from jax.sharding import Mesh, PartitionSpec as P

SPAN = 512
WINDOW = 2048
HD = 192
HID = 768
SHARD = 96
WIDE = 640
BLOCK = 384
SEQ = ("zh", "xy")
AXES = ("zh", "xy", "head")
EPS = 1e-06
LOG2E = 1.4426950408889634
SCORE = math.sqrt(HD)
ROOT_HID = math.sqrt(HID)
BF = jnp.bfloat16
F32 = jnp.float32
VMEM = pl.BlockSpec(memory_space=pltpu.VMEM)
SMEM = pl.BlockSpec(memory_space=pltpu.SMEM)
ANY = pl.BlockSpec(memory_space=pl.ANY)


def pairs(target):
    out = []
    for i in range(256):
        s, h = i // 8, i % 8
        goal = target(s // 16, (s // 4) % 4, s % 4, h // 2, h % 2)
        if goal is not None:
            zh, x, y, zl, c = goal
            out.append((i, ((zh * 4 + x) * 4 + y) * 8 + zl * 2 + c))
    return out


def step_pairs(distance):
    return [(i, ((i // 8 + distance) % 32) * 8 + i % 8) for i in range(256)]


CORE = pairs(lambda zh, x, y, zl, c: (zh, x, y, zl, 1 - c))
ZL1 = pairs(lambda zh, x, y, zl, c: (zh, x, y, zl ^ 1, c))
ZL2 = pairs(lambda zh, x, y, zl, c: (zh, x, y, zl ^ 2, c))
ZL3 = pairs(lambda zh, x, y, zl, c: (zh, x, y, zl ^ 3, c))
ZH = pairs(lambda zh, x, y, zl, c: (1 - zh, x, y, zl, c))
XS = [pairs(lambda zh, x, y, zl, c, k=k: (zh, (x + k) % 4, y, zl, c)) for k in range(4)]
YS = [pairs(lambda zh, x, y, zl, c, k=k: (zh, x, (y + k) % 4, zl, c)) for k in range(4)]
FORWARD = step_pairs(1)
BACK = step_pairs(-1)


def move(array, route):
    return lax.ppermute(array, AXES, route)


def gather_tokens(block):
    near = move(block, CORE)
    one = move(block, ZL1)
    two = move(block, ZL2)
    three = move(two, ZL1)
    return [block, near, one, move(one, CORE), two, move(two, CORE), three, move(three, CORE)]


def matmul(a, b):
    return jnp.dot(a, b, preferred_element_type=F32)


def matmul_nt(a, b):
    return lax.dot_general(a, b, (((1,), (1,)), ((), ())), preferred_element_type=F32)


def unit(rows):
    return rows * lax.rsqrt(jnp.mean(rows * rows, axis=-1, keepdims=True) + EPS)


def sigmoid(a):
    return 1.0 / (1.0 + jnp.exp(-a))


def with_ones(values):
    rows = values.shape[0]
    lane = lax.broadcasted_iota(jnp.int32, (rows, 64), 1)
    return jnp.concatenate([values.astype(F32), jnp.where(lane == 0, 1.0, 0.0)], axis=1).astype(BF)


def call(kernel, outs, *args, flops=0, moved=0, scratch=(), limit=40, after=0, place=VMEM):
    return pl.pallas_call(
        kernel,
        out_shape=outs,
        in_specs=[SMEM] + [VMEM] * (len(args) - 1 - after) + [ANY] * after,
        out_specs=jax.tree.map(lambda _: place, outs),
        scratch_shapes=list(scratch),
        compiler_params=pltpu.CompilerParams(vmem_limit_bytes=limit * 1024 * 1024),
        cost_estimate=pl.CostEstimate(flops=flops, bytes_accessed=moved, transcendentals=0),
    )(*args)


def shape(*dims, dtype=BF):
    return jax.ShapeDtypeStruct(dims, dtype)


def prepare_window(begins, keys, values, unit_keys, wide_values):
    k = keys[...].astype(F32)
    unit_keys[...] = (k * lax.rsqrt(jnp.mean(k * k, axis=0, keepdims=True) + EPS)).astype(BF)
    wide_values[:HD, :] = values[...]
    row = lax.broadcasted_iota(jnp.int32, (64, WINDOW), 0)
    wide_values[HD:, :] = jnp.where(row == 0, 1.0, 0.0).astype(BF)


def build_shard(begins, weight, out):
    for c in range(3):
        out[:, c * HD : (c + 1) * HD] = weight[c]
    out[:, 3 * HD :] = jnp.zeros((SHARD, WIDE - 3 * HD), BF)


def join(begins, *refs):
    out = refs[-1]
    rows = refs[0].shape[0]
    for b, ref in enumerate(refs[:-1]):
        out[b * rows : (b + 1) * rows, :] = ref[...]


def join_column(begins, *refs):
    join(begins, *refs[:4], refs[-1])


def copy_rows(begins, rows, done, first, second):
    first[...] = rows[:SPAN, :]
    second[...] = rows[SPAN:, :]


def pack_state(begins, fast, momentum, out):
    for b in range(8):
        out[b] = fast[24 * b : 24 * (b + 1), :].astype(BF)
        out[8 + b] = momentum[24 * b : 24 * (b + 1), :].astype(BF)


def turn(begins, shares, other, done, done_too, out):
    out[0] = other[...]
    for b in range(15):
        out[b + 1] = shares[b]


def split_out(begins, weight, *refs):
    outs = refs[1:]
    zl = lax.axis_index("head") // 2
    for k in range(4):
        at = pl.multiple_of((zl ^ k) * 2 * BLOCK, 2 * BLOCK)
        outs[k][...] = weight[:, pl.ds(at, 2 * BLOCK)]


def sort_out(begins, *refs):
    mine, theirs = refs[5:]
    core = lax.axis_index("head") % 2
    for k in range(4):
        rows = slice(k * HD, (k + 1) * HD)
        for out, side in ((mine, core), (theirs, 1 - core)):
            out[rows, :] = refs[k][:, pl.ds(pl.multiple_of(side * BLOCK, BLOCK), BLOCK)]


def collect(begins, one, two, three, done, out):
    out[0] = one[...]
    out[1] = two[...]
    out[2] = three[...]


def finish_projection(tokens, weights, rates, queries, keys_grads, values_wide):
    product = matmul(tokens, weights)
    rate = matmul_nt(tokens, rates)[:, :1]
    q = product[:, :HD].astype(BF).astype(F32)
    k = product[:, HD : 2 * HD].astype(BF).astype(F32)
    v = product[:, 2 * HD : 3 * HD].astype(BF)
    soft = jnp.maximum(rate, 0.0) + jnp.log(1.0 + jnp.exp(-jnp.abs(rate)))
    step = (0.3 * soft).astype(BF).astype(F32)
    grad = -step * v.astype(F32)
    queries[...] = unit(q).astype(BF)
    keys_grads[...] = jnp.concatenate([unit(k), grad], axis=1).astype(BF)
    values_wide[...] = with_ones(v)


def load_tokens(blocks, tokens):
    for b, block in enumerate(blocks):
        tokens[:, b * BLOCK : (b + 1) * BLOCK] = block[...]


def project_first(begins, rate, *refs):
    blocks = refs[:8]
    pieces = refs[8:13]
    weights, rates, queries, keys_grads, values_wide, tokens = refs[13:]
    seq, head = lax.axis_index(SEQ), lax.axis_index("head")
    zh, x, y = seq // 16, (seq // 4) % 4, seq % 4
    for dx, piece, base in zip((0, 1, 3, 2, 2), pieces, (0, 0, 0, 0, 2)):
        for dy in range(base, base + piece.shape[0] // (2 * SHARD)):
            from_x, from_y = (x + 4 - dx) % 4, (y + 4 - dy) % 4
            for side in range(2):
                from_zh = zh if side == 0 else 1 - zh
                slot = (from_zh * 4 + from_x) ^ head
                row = pl.multiple_of((slot * 4 + from_y) * SHARD, SHARD)
                at = (2 * (dy - base) + side) * SHARD
                weights[pl.ds(row, SHARD), :] = piece[at : at + SHARD, :]
    rates[...] = jnp.zeros_like(rates)
    for slot in range(8):
        source = pl.multiple_of((slot ^ head) * BLOCK, BLOCK)
        rates[:1, slot * BLOCK : (slot + 1) * BLOCK] = rate[:, pl.ds(source, BLOCK)]
    load_tokens(blocks, tokens)
    finish_projection(
        tokens[...], weights[...], rates[...], queries, keys_grads, values_wide
    )


def project_second(begins, weights, rates, *refs):
    blocks = refs[:8]
    queries, keys_grads, values_wide, tokens = refs[8:]
    load_tokens(blocks, tokens)
    finish_projection(
        tokens[...], weights[...], rates[...], queries, keys_grads, values_wide
    )


def soft_weights(scores, keep=None):
    soft = jnp.exp2(scores * (LOG2E / SCORE) - SCORE * LOG2E)
    if keep is not None:
        soft = jnp.where(keep, soft, 0.0)
    return soft.astype(BF)


def corner(row0, own):
    a = lax.broadcasted_iota(jnp.int32, (256, SPAN), 0) + row0
    j = lax.broadcasted_iota(jnp.int32, (256, SPAN), 1)
    return j <= a if own else j > a


def attend_past(q, row0, keys, values, first):
    total = None
    for at in range(first, WINDOW, SPAN):
        cols = slice(at, at + SPAN)
        keep = corner(row0, False) if at == first else None
        part = matmul_nt(soft_weights(matmul(q, keys[:, cols]), keep), values[:, cols])
        total = part if total is None else total + part
    return total


def attend_own(q, row0, keys, values, causal):
    keep = corner(row0, True) if causal else None
    return matmul(soft_weights(matmul_nt(q, keys), keep), values)


def fast_read(q, weights):
    total = None
    for at in range(0, HID, 256):
        gate = matmul(q, weights(at)) * (1.0 / SCORE)
        lift = matmul(q, weights(HID + at)) * (1.0 / SCORE)
        hidden = (gate * sigmoid(gate) * lift).astype(BF)
        part = matmul_nt(hidden, weights(2 * HID + at))
        total = part if total is None else total + part
    return total * (1.0 / ROOT_HID)


def fast_write(keys_grads, weights, momentum, weights_out, momentum_out):
    y = keys_grads[:, :HD]
    g = keys_grads[:, HD:]
    y_turned = y.astype(F32).T.astype(BF)
    g_turned = g.astype(F32).T.astype(BF)
    for at in range(0, HID, 256):
        spots = (at, HID + at, 2 * HID + at)
        now = [weights(spot) for spot in spots]
        u1, u3, p = (w.astype(BF) for w in now)
        gate = matmul(y, u1) * (1.0 / SCORE)
        lift = matmul(y, u3) * (1.0 / SCORE)
        err = matmul(g, p) * (1.0 / ROOT_HID)
        sg = sigmoid(gate)
        silu = gate * sg
        gate_grad = (err * lift * sg * (1.0 + gate * (1.0 - sg))).astype(BF)
        lift_grad = (err * silu).astype(BF)
        hidden = (silu * lift).astype(BF)
        grads = (
            matmul(y_turned, gate_grad) * (1.0 / SCORE),
            matmul(y_turned, lift_grad) * (1.0 / SCORE),
            matmul(g_turned, hidden) * (1.0 / ROOT_HID),
        )
        for spot, w, grad in zip(spots, now, grads):
            m = 0.9 * momentum(spot) + grad
            stepped = w - m
            scale = lax.rsqrt(jnp.mean(stepped * stepped, axis=0, keepdims=True) + EPS)
            weights_out(spot, stepped * scale)
            momentum_out(spot, m)


def first_mix(begins, queries, keys_grads, values, past_keys, past_values, fast_far, initial_far, mix, fast, initial, arrived):
    copies = [
        pltpu.make_async_copy(fast_far, fast, arrived.at[0]),
        pltpu.make_async_copy(initial_far, initial, arrived.at[1]),
    ]
    for copy in copies:
        copy.start()
    fresh = begins[0, lax.axis_index(SEQ)] > 0
    seen = jnp.where(fresh, 0.0, 1.0)
    for row in range(0, SPAN, 256):
        q = queries[row : row + 256, :]
        past = attend_past(q, row, past_keys, past_values, 0)
        own = attend_own(q, row, keys_grads[:, :HD], values[...], True)
        total = past * seen + own
        attended = total[:, :HD] / total[:, HD : HD + 1]
        if row == 0:
            for copy in copies:
                copy.wait()
        applied = fast_read(
            q,
            lambda at: jnp.where(
                fresh, initial[:, at : at + 256].astype(F32), fast[:, at : at + 256]
            ).astype(BF),
        )
        mix[:, row : row + 256] = (attended + applied).T.astype(BF)


def lend_window(begins, queries, past_keys, past_values, keys_grads, values, mix, part):
    seq = lax.axis_index(SEQ)
    old = jnp.where(begins[0, seq] > 0, 0.0, 1.0)
    seen = jnp.where(begins[1, (seq + 1) % 32] > 0, 0.0, 1.0)
    for row in range(0, SPAN, 256):
        q = queries[row : row + 256, :]
        past = attend_past(q, row, past_keys, past_values, SPAN)
        new = attend_own(q, row, keys_grads[:, :HD], values[...], False)
        total = (past * old + new) * seen
        weight = total[:, HD : HD + 1]
        high = weight.astype(BF).astype(F32)
        lane = lax.broadcasted_iota(jnp.int32, (256, 64), 1)
        tail = jnp.where(lane == 0, high, jnp.where(lane == 1, weight - high, 0.0))
        part[row : row + 256, :] = jnp.concatenate([total[:, :HD], tail], axis=1).astype(BF)


def arrive_state(begins, keys_grads, state, initial, fast_out, momentum_out):
    seq = lax.axis_index(SEQ)
    fresh_before = begins[0, (seq + 31) % 32] > 0
    fresh = begins[1, seq] > 0

    def rows_of(first, at):
        return jnp.concatenate(
            [state[first + b, :, at : at + 256].astype(F32) for b in range(8)], axis=0
        )

    def weights(at):
        return jnp.where(
            fresh_before,
            initial[:, at : at + 256].astype(F32),
            rows_of(0, at),
        )

    def moment(at):
        return jnp.where(fresh_before, 0.0, rows_of(8, at))

    def keep_weights(at, value):
        fast_out[:, at : at + 256] = jnp.where(
            fresh, initial[:, at : at + 256].astype(F32), value
        )

    def keep_moment(at, value):
        momentum_out[:, at : at + 256] = jnp.where(fresh, 0.0, value)

    fast_write(keys_grads, weights, moment, keep_weights, keep_moment)


def second_mix(begins, queries, keys_grads, values, fast, part, mix):
    for row in range(0, SPAN, 256):
        rows = slice(row, row + 256)
        q = queries[rows, :]
        total = attend_own(q, row, keys_grads[:, :HD], values[...], True)
        lent = part[rows, :].astype(F32)
        weight = total[:, HD : HD + 1] + lent[:, HD : HD + 1] + lent[:, HD + 1 : HD + 2]
        attended = (total[:, :HD] + lent[:, :HD]) / weight
        applied = fast_read(q, lambda at: fast[:, at : at + 256].astype(BF))
        mix[:, rows] = (attended + applied).T.astype(BF)


def last_state(
    begins, keys_grads, fast, momentum, fast_far, momentum_far, fast_out, momentum_out, sent
):
    def keep_weights(at, value):
        fast_out[:, at : at + 256] = value

    def keep_moment(at, value):
        momentum_out[:, at : at + 256] = value

    fast_write(
        keys_grads,
        lambda at: fast[:, at : at + 256],
        lambda at: momentum[:, at : at + 256],
        keep_weights,
        keep_moment,
    )
    copies = [
        pltpu.make_async_copy(fast_out, fast_far, sent.at[0]),
        pltpu.make_async_copy(momentum_out, momentum_far, sent.at[1]),
    ]
    for copy in copies:
        copy.start()
    for copy in copies:
        copy.wait()


def matmul_tn(a, b):
    return lax.dot_general(a, b, (((0,), (0,)), ((), ())), preferred_element_type=F32)


def project_mix(own, near, got, near_got, mine, theirs):
    total = matmul_tn(own[...], mine[:HD, :]) + matmul_tn(near[...], theirs[:HD, :])
    for k in (1, 2, 3):
        rows = slice(k * HD, (k + 1) * HD)
        total = total + matmul_tn(got[k - 1], mine[rows, :])
        total = total + matmul_tn(near_got[k - 1], theirs[rows, :])
    return total.astype(BF)


def project_out_first(begins, own, near, got, near_got, mine, theirs, done, out):
    out[...] = project_mix(own, near, got, near_got, mine, theirs)


def project_out_last(begins, own, near, got, near_got, mine, theirs, earlier, out):
    out[:SPAN, :] = earlier[...]
    out[SPAN:, :] = project_mix(own, near, got, near_got, mine, theirs)


def body(
    tokens,
    fast_state,
    momentum,
    init_fast,
    past_keys,
    past_values,
    qkv_weight,
    rate_weight,
    out_weight,
    prompt_begins,
):
    seq = lax.axis_index(SEQ)
    shard = call(build_shard, shape(SHARD, WIDE), prompt_begins, qkv_weight)
    across = move(shard, ZH)
    pair = call(join, shape(2 * SHARD, WIDE), prompt_begins, shard, across)
    token_rows = call(
        copy_rows,
        (shape(SPAN, BLOCK), shape(SPAN, BLOCK)),
        prompt_begins,
        tokens[0],
        across,
        after=1,
    )
    first_tokens, second_tokens = (gather_tokens(rows) for rows in token_rows)
    column = call(
        join_column,
        shape(8 * SHARD, WIDE),
        prompt_begins,
        pair,
        *[move(pair, YS[k]) for k in (1, 2, 3)],
        first_tokens[2],
        first_tokens[4],
        after=2,
    )
    left = move(column, XS[1])
    right = move(column, XS[3])
    pieces = [column, left, right, move(left[:384], XS[1]), move(right[384:], XS[3])]
    state = call(
        pack_state,
        shape(16, 24, 3 * HID),
        prompt_begins,
        fast_state[0, 0],
        momentum[0, 0],
    )
    shares = lax.all_to_all(state, "xy", 0, 0, tiled=False)
    shares = call(
        turn,
        shape(16, 24, 3 * HID),
        prompt_begins,
        shares,
        move(shares[15], ZH),
        pieces[3],
        pieces[4],
        after=2,
    )
    state_sent = lax.all_to_all(shares, "xy", 0, 0, tiled=False)
    unit_keys, wide_values = call(
        prepare_window,
        (shape(HD, WINDOW), shape(256, WINDOW)),
        prompt_begins,
        past_keys[0].T,
        past_values[0].T,
        moved=4 << 20,
    )
    span_outs = (shape(SPAN, HD), shape(SPAN, 2 * HD), shape(SPAN, 256))
    token_room = pltpu.VMEM((SPAN, 8 * BLOCK), BF)
    weights, rates, q0, kg0, v0 = call(
        project_first,
        (shape(8 * BLOCK, WIDE), shape(16, 8 * BLOCK)) + span_outs,
        prompt_begins,
        rate_weight.T,
        *first_tokens,
        *pieces,
        flops=2 * SPAN * 3072 * WIDE,
        moved=12 << 20,
        scratch=[token_room],
    )
    kg_before = move(kg0, FORWARD)
    out_parts = call(
        split_out,
        tuple(shape(HD, 2 * BLOCK) for _ in range(4)),
        prompt_begins,
        out_weight,
        q0,
        after=1,
    )
    out_parts = [out_parts[0]] + [
        move(part, route) for part, route in zip(out_parts[1:], (ZL1, ZL2, ZL3))
    ]
    mix0 = call(
        first_mix,
        shape(HD, SPAN),
        prompt_begins,
        q0,
        kg0,
        v0,
        unit_keys,
        wide_values,
        fast_state[0, 0],
        init_fast[0],
        flops=4 << 30,
        moved=6 << 20,
        after=2,
        scratch=[
            pltpu.VMEM((HD, 3 * HID), F32),
            pltpu.VMEM((HD, 3 * HID), BF),
            pltpu.SemaphoreType.DMA((2,)),
        ],
    )

    q1, kg1, v1 = call(
        project_second,
        span_outs,
        prompt_begins,
        weights,
        rates,
        *second_tokens,
        flops=2 * SPAN * 3072 * WIDE,
        moved=8 << 20,
        scratch=[token_room],
    )
    q_next = move(q1, BACK)
    part = call(
        lend_window,
        shape(SPAN, 256),
        prompt_begins,
        q_next,
        unit_keys,
        wide_values,
        kg0,
        v0,
        mix0,
        flops=3 << 30,
        moved=3 << 20,
        after=1,
    )
    part_before = move(part, FORWARD)
    state = shape(HD, 3 * HID, dtype=F32)
    fast1, momentum1 = call(
        arrive_state,
        (state, state),
        prompt_begins,
        kg_before,
        state_sent,
        init_fast[0],
        flops=3 << 30,
        moved=6 << 20,
    )
    out_mine, out_theirs = call(
        sort_out,
        (shape(4 * HD, BLOCK), shape(4 * HD, BLOCK)),
        prompt_begins,
        *out_parts,
        fast1,
        after=1,
    )
    out_rows = (out_mine, move(out_theirs, CORE))

    def gather_mix(mix, done):
        near = move(mix, CORE)
        got = call(
            collect,
            shape(3, HD, SPAN),
            prompt_begins,
            *[move(mix, route) for route in (ZL1, ZL2, ZL3)],
            done,
            after=1,
        )
        return (mix, near, got, move(got, CORE)) + out_rows

    cost = dict(flops=2 * SPAN * 1536 * BLOCK, moved=4 << 20)
    mix1 = call(
        second_mix,
        shape(HD, SPAN),
        prompt_begins,
        q1,
        kg1,
        v1,
        fast1,
        part_before,
        flops=2 << 30,
        moved=3 << 20,
    )
    fast2, momentum2 = call(
        last_state,
        (state, state),
        prompt_begins,
        kg1,
        fast1,
        momentum1,
        flops=3 << 30,
        moved=8 << 20,
        place=ANY,
        scratch=[
            pltpu.VMEM((HD, 3 * HID), F32),
            pltpu.VMEM((HD, 3 * HID), F32),
            pltpu.SemaphoreType.DMA((2,)),
        ],
    )
    mix0_all = gather_mix(mix0, fast1)
    out0 = call(
        project_out_first,
        shape(SPAN, BLOCK),
        prompt_begins,
        *mix0_all,
        mix1,
        after=1,
        **cost,
    )
    mix1_all = gather_mix(mix1, fast2)
    mixed = call(
        project_out_last, shape(2 * SPAN, BLOCK), prompt_begins, *mix1_all, out0, **cost
    )
    return mixed[None], fast2[None, None], momentum2[None, None]


def solution(mesh):
    in_specs = (
        P(SEQ, None, "head"),
        P(SEQ, "head", None, None),
        P(SEQ, "head", None, None),
        P("head", None, None),
        P(SEQ, None, "head"),
        P(SEQ, None, "head"),
        P(None, SEQ, "head"),
        P(None, "head"),
        P("head", None),
        P(),
    )
    out_specs = (P(SEQ, None, "head"), P(SEQ, "head", None, None), P(SEQ, "head", None, None))
    mesh = Mesh(mesh.devices.reshape(2, 16, 8), AXES)
    return jax.shard_map(body, mesh=mesh, in_specs=in_specs, out_specs=out_specs, check_vma=False)
```

```python
import math

import jax
import jax.numpy as jnp
from jax import lax
from jax.experimental import pallas as pl
from jax.experimental.pallas import tpu as pltpu
from jax.sharding import Mesh, PartitionSpec as P

SPAN = 512
WINDOW = 2048
HD = 192
HID = 768
SHARD = 96
WIDE = 640
BLOCK = 384
SEQ = ("zh", "xy")
AXES = ("zh", "xy", "head")
EPS = 1e-06
LOG2E = 1.4426950408889634
SCORE = math.sqrt(HD)
ROOT_HID = math.sqrt(HID)
BF = jnp.bfloat16
F32 = jnp.float32
VMEM = pl.BlockSpec(memory_space=pltpu.VMEM)
SMEM = pl.BlockSpec(memory_space=pltpu.SMEM)
ANY = pl.BlockSpec(memory_space=pl.ANY)


def pairs(target):
    out = []
    for i in range(256):
        s, h = i // 8, i % 8
        goal = target(s // 16, (s // 4) % 4, s % 4, h // 2, h % 2)
        if goal is not None:
            zh, x, y, zl, c = goal
            out.append((i, ((zh * 4 + x) * 4 + y) * 8 + zl * 2 + c))
    return out


def step_pairs(distance):
    return [(i, ((i // 8 + distance) % 32) * 8 + i % 8) for i in range(256)]


CORE = pairs(lambda zh, x, y, zl, c: (zh, x, y, zl, 1 - c))
ZL1 = pairs(lambda zh, x, y, zl, c: (zh, x, y, zl ^ 1, c))
ZL2 = pairs(lambda zh, x, y, zl, c: (zh, x, y, zl ^ 2, c))
ZL3 = pairs(lambda zh, x, y, zl, c: (zh, x, y, zl ^ 3, c))
ZH = pairs(lambda zh, x, y, zl, c: (1 - zh, x, y, zl, c))
XS = [pairs(lambda zh, x, y, zl, c, k=k: (zh, (x + k) % 4, y, zl, c)) for k in range(4)]
YS = [pairs(lambda zh, x, y, zl, c, k=k: (zh, x, (y + k) % 4, zl, c)) for k in range(4)]
FORWARD = step_pairs(1)
BACK = step_pairs(-1)


def move(array, route):
    return lax.ppermute(array, AXES, route)


def gather_tokens(block):
    near = move(block, CORE)
    one = move(block, ZL1)
    two = move(block, ZL2)
    three = move(two, ZL1)
    return [block, near, one, move(one, CORE), two, move(two, CORE), three, move(three, CORE)]


def matmul(a, b):
    return jnp.dot(a, b, preferred_element_type=F32)


def matmul_nt(a, b):
    return lax.dot_general(a, b, (((1,), (1,)), ((), ())), preferred_element_type=F32)


def unit(rows):
    return rows * lax.rsqrt(jnp.mean(rows * rows, axis=-1, keepdims=True) + EPS)


def sigmoid(a):
    return 1.0 / (1.0 + jnp.exp(-a))


def with_ones(values):
    rows = values.shape[0]
    lane = lax.broadcasted_iota(jnp.int32, (rows, 64), 1)
    return jnp.concatenate([values.astype(F32), jnp.where(lane == 0, 1.0, 0.0)], axis=1).astype(BF)


def call(kernel, outs, *args, flops=0, moved=0, scratch=(), limit=40, after=0, place=VMEM):
    return pl.pallas_call(
        kernel,
        out_shape=outs,
        in_specs=[SMEM] + [VMEM] * (len(args) - 1 - after) + [ANY] * after,
        out_specs=jax.tree.map(lambda _: place, outs),
        scratch_shapes=list(scratch),
        compiler_params=pltpu.CompilerParams(vmem_limit_bytes=limit * 1024 * 1024),
        cost_estimate=pl.CostEstimate(flops=flops, bytes_accessed=moved, transcendentals=0),
    )(*args)


def shape(*dims, dtype=BF):
    return jax.ShapeDtypeStruct(dims, dtype)


def prepare_window(begins, keys, values, unit_keys, wide_values):
    k = keys[...].astype(F32)
    unit_keys[...] = (k * lax.rsqrt(jnp.mean(k * k, axis=0, keepdims=True) + EPS)).astype(BF)
    wide_values[:HD, :] = values[...]
    row = lax.broadcasted_iota(jnp.int32, (64, WINDOW), 0)
    wide_values[HD:, :] = jnp.where(row == 0, 1.0, 0.0).astype(BF)


def build_shard(begins, weight, out):
    for c in range(3):
        out[:, c * HD : (c + 1) * HD] = weight[c]
    out[:, 3 * HD :] = jnp.zeros((SHARD, WIDE - 3 * HD), BF)


def join(begins, *refs):
    out = refs[-1]
    rows = refs[0].shape[0]
    for b, ref in enumerate(refs[:-1]):
        out[b * rows : (b + 1) * rows, :] = ref[...]


def join_column(begins, *refs):
    join(begins, *refs[:4], refs[-1])


def copy_rows(begins, rows, done, first, second):
    first[...] = rows[:SPAN, :]
    second[...] = rows[SPAN:, :]


def pack_state(begins, fast, momentum, out):
    for b in range(8):
        out[b] = fast[24 * b : 24 * (b + 1), :].astype(BF)
        out[8 + b] = momentum[24 * b : 24 * (b + 1), :].astype(BF)


def turn(begins, shares, other, done, done_too, out):
    out[0] = other[...]
    for b in range(15):
        out[b + 1] = shares[b]


def split_out(begins, weight, *refs):
    outs = refs[1:]
    zl = lax.axis_index("head") // 2
    for k in range(4):
        at = pl.multiple_of((zl ^ k) * 2 * BLOCK, 2 * BLOCK)
        outs[k][...] = weight[:, pl.ds(at, 2 * BLOCK)]


def sort_out(begins, *refs):
    mine, theirs = refs[4:]
    core = lax.axis_index("head") % 2
    for k in range(4):
        rows = slice(k * HD, (k + 1) * HD)
        for out, side in ((mine, core), (theirs, 1 - core)):
            out[rows, :] = refs[k][:, pl.ds(pl.multiple_of(side * BLOCK, BLOCK), BLOCK)]


def collect(begins, one, two, three, done, out):
    out[0] = one[...]
    out[1] = two[...]
    out[2] = three[...]


def finish_projection(tokens, weights, rates, queries, keys_grads, values_wide):
    product = matmul(tokens, weights)
    rate = matmul_nt(tokens, rates)[:, :1]
    q = product[:, :HD].astype(BF).astype(F32)
    k = product[:, HD : 2 * HD].astype(BF).astype(F32)
    v = product[:, 2 * HD : 3 * HD].astype(BF)
    soft = jnp.maximum(rate, 0.0) + jnp.log(1.0 + jnp.exp(-jnp.abs(rate)))
    step = (0.3 * soft).astype(BF).astype(F32)
    grad = -step * v.astype(F32)
    queries[...] = unit(q).astype(BF)
    keys_grads[...] = jnp.concatenate([unit(k), grad], axis=1).astype(BF)
    values_wide[...] = with_ones(v)


def load_tokens(blocks, tokens):
    for b, block in enumerate(blocks):
        tokens[:, b * BLOCK : (b + 1) * BLOCK] = block[...]


def project_first(begins, rate, *refs):
    blocks = refs[:8]
    pieces = refs[8:13]
    weights, rates, queries, keys_grads, values_wide, tokens = refs[13:]
    seq, head = lax.axis_index(SEQ), lax.axis_index("head")
    zh, x, y = seq // 16, (seq // 4) % 4, seq % 4
    for dx, piece, base in zip((0, 1, 3, 2, 2), pieces, (0, 0, 0, 0, 2)):
        for dy in range(base, base + piece.shape[0] // (2 * SHARD)):
            from_x, from_y = (x + 4 - dx) % 4, (y + 4 - dy) % 4
            for side in range(2):
                from_zh = zh if side == 0 else 1 - zh
                slot = (from_zh * 4 + from_x) ^ head
                row = pl.multiple_of((slot * 4 + from_y) * SHARD, SHARD)
                at = (2 * (dy - base) + side) * SHARD
                weights[pl.ds(row, SHARD), :] = piece[at : at + SHARD, :]
    rates[...] = jnp.zeros_like(rates)
    for slot in range(8):
        source = pl.multiple_of((slot ^ head) * BLOCK, BLOCK)
        rates[:1, slot * BLOCK : (slot + 1) * BLOCK] = rate[:, pl.ds(source, BLOCK)]
    load_tokens(blocks, tokens)
    finish_projection(
        tokens[...], weights[...], rates[...], queries, keys_grads, values_wide
    )


def project_second(begins, weights, rates, *refs):
    blocks = refs[:8]
    queries, keys_grads, values_wide, tokens = refs[8:]
    load_tokens(blocks, tokens)
    finish_projection(
        tokens[...], weights[...], rates[...], queries, keys_grads, values_wide
    )


def soft_weights(scores, keep=None):
    soft = jnp.exp2(scores * (LOG2E / SCORE) - SCORE * LOG2E)
    if keep is not None:
        soft = jnp.where(keep, soft, 0.0)
    return soft.astype(BF)


def corner(row0, own):
    a = lax.broadcasted_iota(jnp.int32, (256, SPAN), 0) + row0
    j = lax.broadcasted_iota(jnp.int32, (256, SPAN), 1)
    return j <= a if own else j > a


def attend_past(q, row0, keys, values, first):
    total = None
    for at in range(first, WINDOW, SPAN):
        cols = slice(at, at + SPAN)
        keep = corner(row0, False) if at == first else None
        part = matmul_nt(soft_weights(matmul(q, keys[:, cols]), keep), values[:, cols])
        total = part if total is None else total + part
    return total


def attend_own(q, row0, keys, values, causal):
    keep = corner(row0, True) if causal else None
    return matmul(soft_weights(matmul_nt(q, keys), keep), values)


def fast_read(q, weights):
    total = None
    for at in range(0, HID, 256):
        gate = matmul(q, weights(at)) * (1.0 / SCORE)
        lift = matmul(q, weights(HID + at)) * (1.0 / SCORE)
        hidden = (gate * sigmoid(gate) * lift).astype(BF)
        part = matmul_nt(hidden, weights(2 * HID + at))
        total = part if total is None else total + part
    return total * (1.0 / ROOT_HID)


def fast_write(keys_grads, weights, momentum, weights_out, momentum_out):
    y = keys_grads[:, :HD]
    g = keys_grads[:, HD:]
    y_turned = y.astype(F32).T.astype(BF)
    g_turned = g.astype(F32).T.astype(BF)
    for at in range(0, HID, 256):
        spots = (at, HID + at, 2 * HID + at)
        now = [weights(spot) for spot in spots]
        u1, u3, p = (w.astype(BF) for w in now)
        gate = matmul(y, u1) * (1.0 / SCORE)
        lift = matmul(y, u3) * (1.0 / SCORE)
        err = matmul(g, p) * (1.0 / ROOT_HID)
        sg = sigmoid(gate)
        silu = gate * sg
        gate_grad = (err * lift * sg * (1.0 + gate * (1.0 - sg))).astype(BF)
        lift_grad = (err * silu).astype(BF)
        hidden = (silu * lift).astype(BF)
        grads = (
            matmul(y_turned, gate_grad) * (1.0 / SCORE),
            matmul(y_turned, lift_grad) * (1.0 / SCORE),
            matmul(g_turned, hidden) * (1.0 / ROOT_HID),
        )
        for spot, w, grad in zip(spots, now, grads):
            m = 0.9 * momentum(spot) + grad
            stepped = w - m
            scale = lax.rsqrt(jnp.mean(stepped * stepped, axis=0, keepdims=True) + EPS)
            weights_out(spot, stepped * scale)
            momentum_out(spot, m)


def first_mix(begins, queries, keys_grads, values, past_keys, past_values, fast_far, initial_far, done, mix, fast, initial, arrived):
    copies = [
        pltpu.make_async_copy(fast_far, fast, arrived.at[0]),
        pltpu.make_async_copy(initial_far, initial, arrived.at[1]),
    ]
    for copy in copies:
        copy.start()
    fresh = begins[0, lax.axis_index(SEQ)] > 0
    seen = jnp.where(fresh, 0.0, 1.0)
    for row in range(0, SPAN, 256):
        q = queries[row : row + 256, :]
        past = attend_past(q, row, past_keys, past_values, 0)
        own = attend_own(q, row, keys_grads[:, :HD], values[...], True)
        total = past * seen + own
        attended = total[:, :HD] / total[:, HD : HD + 1]
        if row == 0:
            for copy in copies:
                copy.wait()
        applied = fast_read(
            q,
            lambda at: jnp.where(
                fresh, initial[:, at : at + 256].astype(F32), fast[:, at : at + 256]
            ).astype(BF),
        )
        mix[:, row : row + 256] = (attended + applied).T.astype(BF)


def lend_window(begins, queries, past_keys, past_values, keys_grads, values, mix, part):
    seq = lax.axis_index(SEQ)
    old = jnp.where(begins[0, seq] > 0, 0.0, 1.0)
    seen = jnp.where(begins[1, (seq + 1) % 32] > 0, 0.0, 1.0)
    for row in range(0, SPAN, 256):
        q = queries[row : row + 256, :]
        past = attend_past(q, row, past_keys, past_values, SPAN)
        new = attend_own(q, row, keys_grads[:, :HD], values[...], False)
        total = (past * old + new) * seen
        weight = total[:, HD : HD + 1]
        high = weight.astype(BF).astype(F32)
        lane = lax.broadcasted_iota(jnp.int32, (256, 64), 1)
        tail = jnp.where(lane == 0, high, jnp.where(lane == 1, weight - high, 0.0))
        part[row : row + 256, :] = jnp.concatenate([total[:, :HD], tail], axis=1).astype(BF)


def arrive_state(begins, keys_grads, state, initial, fast_out, momentum_out):
    seq = lax.axis_index(SEQ)
    fresh_before = begins[0, (seq + 31) % 32] > 0
    fresh = begins[1, seq] > 0

    def rows_of(first, at):
        return jnp.concatenate(
            [state[first + b, :, at : at + 256].astype(F32) for b in range(8)], axis=0
        )

    def weights(at):
        return jnp.where(
            fresh_before,
            initial[:, at : at + 256].astype(F32),
            rows_of(0, at),
        )

    def moment(at):
        return jnp.where(fresh_before, 0.0, rows_of(8, at))

    def keep_weights(at, value):
        fast_out[:, at : at + 256] = jnp.where(
            fresh, initial[:, at : at + 256].astype(F32), value
        )

    def keep_moment(at, value):
        momentum_out[:, at : at + 256] = jnp.where(fresh, 0.0, value)

    fast_write(keys_grads, weights, moment, keep_weights, keep_moment)


def second_mix(begins, queries, keys_grads, values, fast, part, mix):
    for row in range(0, SPAN, 256):
        rows = slice(row, row + 256)
        q = queries[rows, :]
        total = attend_own(q, row, keys_grads[:, :HD], values[...], True)
        lent = part[rows, :].astype(F32)
        weight = total[:, HD : HD + 1] + lent[:, HD : HD + 1] + lent[:, HD + 1 : HD + 2]
        attended = (total[:, :HD] + lent[:, :HD]) / weight
        applied = fast_read(q, lambda at: fast[:, at : at + 256].astype(BF))
        mix[:, rows] = (attended + applied).T.astype(BF)


def last_state(
    begins, keys_grads, fast, momentum, fast_far, momentum_far, fast_out, momentum_out, sent
):
    def keep_weights(at, value):
        fast_out[:, at : at + 256] = value

    def keep_moment(at, value):
        momentum_out[:, at : at + 256] = value

    fast_write(
        keys_grads,
        lambda at: fast[:, at : at + 256],
        lambda at: momentum[:, at : at + 256],
        keep_weights,
        keep_moment,
    )
    copies = [
        pltpu.make_async_copy(fast_out, fast_far, sent.at[0]),
        pltpu.make_async_copy(momentum_out, momentum_far, sent.at[1]),
    ]
    for copy in copies:
        copy.start()
    for copy in copies:
        copy.wait()


def matmul_tn(a, b):
    return lax.dot_general(a, b, (((0,), (0,)), ((), ())), preferred_element_type=F32)


def project_mix(own, near, got, near_got, mine, theirs):
    total = matmul_tn(own[...], mine[:HD, :]) + matmul_tn(near[...], theirs[:HD, :])
    for k in (1, 2, 3):
        rows = slice(k * HD, (k + 1) * HD)
        total = total + matmul_tn(got[k - 1], mine[rows, :])
        total = total + matmul_tn(near_got[k - 1], theirs[rows, :])
    return total.astype(BF)


def project_out_first(begins, own, near, got, near_got, mine, theirs, done, out):
    out[...] = project_mix(own, near, got, near_got, mine, theirs)


def project_out_last(begins, own, near, got, near_got, mine, theirs, earlier, out):
    out[:SPAN, :] = earlier[...]
    out[SPAN:, :] = project_mix(own, near, got, near_got, mine, theirs)


def body(
    tokens,
    fast_state,
    momentum,
    init_fast,
    past_keys,
    past_values,
    qkv_weight,
    rate_weight,
    out_weight,
    prompt_begins,
):
    seq = lax.axis_index(SEQ)
    shard = call(build_shard, shape(SHARD, WIDE), prompt_begins, qkv_weight)
    across = move(shard, ZH)
    pair = call(join, shape(2 * SHARD, WIDE), prompt_begins, shard, across)
    token_rows = call(
        copy_rows,
        (shape(SPAN, BLOCK), shape(SPAN, BLOCK)),
        prompt_begins,
        tokens[0],
        across,
        after=1,
    )
    first_tokens, second_tokens = (gather_tokens(rows) for rows in token_rows)
    column = call(
        join_column,
        shape(8 * SHARD, WIDE),
        prompt_begins,
        pair,
        *[move(pair, YS[k]) for k in (1, 2, 3)],
        first_tokens[2],
        first_tokens[4],
        after=2,
    )
    left = move(column, XS[1])
    right = move(column, XS[3])
    pieces = [column, left, right, move(left[:384], XS[1]), move(right[384:], XS[3])]
    state = call(
        pack_state,
        shape(16, 24, 3 * HID),
        prompt_begins,
        fast_state[0, 0],
        momentum[0, 0],
    )
    shares = lax.all_to_all(state, "xy", 0, 0, tiled=False)
    shares = call(
        turn,
        shape(16, 24, 3 * HID),
        prompt_begins,
        shares,
        move(shares[15], ZH),
        pieces[3],
        pieces[4],
        after=2,
    )
    state_sent = lax.all_to_all(shares, "xy", 0, 0, tiled=False)
    unit_keys, wide_values = call(
        prepare_window,
        (shape(HD, WINDOW), shape(256, WINDOW)),
        prompt_begins,
        past_keys[0].T,
        past_values[0].T,
        moved=4 << 20,
    )
    span_outs = (shape(SPAN, HD), shape(SPAN, 2 * HD), shape(SPAN, 256))
    token_room = pltpu.VMEM((SPAN, 8 * BLOCK), BF)
    weights, rates, q0, kg0, v0 = call(
        project_first,
        (shape(8 * BLOCK, WIDE), shape(16, 8 * BLOCK)) + span_outs,
        prompt_begins,
        rate_weight.T,
        *first_tokens,
        *pieces,
        flops=2 * SPAN * 3072 * WIDE,
        moved=12 << 20,
        scratch=[token_room],
    )
    kg_before = move(kg0, FORWARD)
    out_parts = call(
        split_out,
        tuple(shape(HD, 2 * BLOCK) for _ in range(4)),
        prompt_begins,
        out_weight,
        q0,
        after=1,
    )
    out_parts = [out_parts[0]] + [
        move(part, route) for part, route in zip(out_parts[1:], (ZL1, ZL2, ZL3))
    ]
    out_mine, out_theirs = call(
        sort_out,
        (shape(4 * HD, BLOCK), shape(4 * HD, BLOCK)),
        prompt_begins,
        *out_parts,
    )
    out_rows = (out_mine, move(out_theirs, CORE))
    mix0 = call(
        first_mix,
        shape(HD, SPAN),
        prompt_begins,
        q0,
        kg0,
        v0,
        unit_keys,
        wide_values,
        fast_state[0, 0],
        init_fast[0],
        out_mine,
        flops=4 << 30,
        moved=6 << 20,
        after=3,
        scratch=[
            pltpu.VMEM((HD, 3 * HID), F32),
            pltpu.VMEM((HD, 3 * HID), BF),
            pltpu.SemaphoreType.DMA((2,)),
        ],
    )

    q1, kg1, v1 = call(
        project_second,
        span_outs,
        prompt_begins,
        weights,
        rates,
        *second_tokens,
        flops=2 * SPAN * 3072 * WIDE,
        moved=8 << 20,
        scratch=[token_room],
    )
    q_next = move(q1, BACK)
    part = call(
        lend_window,
        shape(SPAN, 256),
        prompt_begins,
        q_next,
        unit_keys,
        wide_values,
        kg0,
        v0,
        mix0,
        flops=3 << 30,
        moved=3 << 20,
        after=1,
    )
    part_before = move(part, FORWARD)
    state = shape(HD, 3 * HID, dtype=F32)
    fast1, momentum1 = call(
        arrive_state,
        (state, state),
        prompt_begins,
        kg_before,
        state_sent,
        init_fast[0],
        flops=3 << 30,
        moved=6 << 20,
    )

    def gather_mix(mix, done):
        near = move(mix, CORE)
        got = call(
            collect,
            shape(3, HD, SPAN),
            prompt_begins,
            *[move(mix, route) for route in (ZL1, ZL2, ZL3)],
            done,
            after=1,
        )
        return (mix, near, got, move(got, CORE)) + out_rows

    cost = dict(flops=2 * SPAN * 1536 * BLOCK, moved=4 << 20)
    mix1 = call(
        second_mix,
        shape(HD, SPAN),
        prompt_begins,
        q1,
        kg1,
        v1,
        fast1,
        part_before,
        flops=2 << 30,
        moved=3 << 20,
    )
    fast2, momentum2 = call(
        last_state,
        (state, state),
        prompt_begins,
        kg1,
        fast1,
        momentum1,
        flops=3 << 30,
        moved=8 << 20,
        place=ANY,
        scratch=[
            pltpu.VMEM((HD, 3 * HID), F32),
            pltpu.VMEM((HD, 3 * HID), F32),
            pltpu.SemaphoreType.DMA((2,)),
        ],
    )
    mix0_all = gather_mix(mix0, fast1)
    out0 = call(
        project_out_first,
        shape(SPAN, BLOCK),
        prompt_begins,
        *mix0_all,
        mix1,
        after=1,
        **cost,
    )
    mix1_all = gather_mix(mix1, fast2)
    mixed = call(
        project_out_last, shape(2 * SPAN, BLOCK), prompt_begins, *mix1_all, out0, **cost
    )
    return mixed[None], fast2[None, None], momentum2[None, None]


def solution(mesh):
    in_specs = (
        P(SEQ, None, "head"),
        P(SEQ, "head", None, None),
        P(SEQ, "head", None, None),
        P("head", None, None),
        P(SEQ, None, "head"),
        P(SEQ, None, "head"),
        P(None, SEQ, "head"),
        P(None, "head"),
        P("head", None),
        P(),
    )
    out_specs = (P(SEQ, None, "head"), P(SEQ, "head", None, None), P(SEQ, "head", None, None))
    mesh = Mesh(mesh.devices.reshape(2, 16, 8), AXES)
    return jax.shard_map(body, mesh=mesh, in_specs=in_specs, out_specs=out_specs, check_vma=False)
```
